128 devices in a mesh: replica: 8 (over y, z_hi), dp: 16 (over z_lo, x, core).
Axes of the slice: x: 4, y: 4, z: 4 (z_hi: 2, z_lo: 2; z = z_hi * 2 + z_lo), core: 2. Of those that a mesh axis runs over, the one named last changes fastest.
Arguments:
- tokens: bfloat16 [32768, 1152], P(('replica', 'dp')), may hold values from -6 to 6
- hidden: bfloat16 [32768, 4304], P(('replica', 'dp')), may hold values from -6 to 6
- w_out: bfloat16 [1152, 4304], replicated, may hold values from -0.09375 to 0.09375
- norm_gain: float32 [1152], replicated, may hold values from 0.1 to 1.9
- text_embed: bfloat16 [128, 1152], P(('replica', 'dp')), may hold values from -6 to 6
- logit_scale: float32 [1], replicated, may hold values from 4 to 16
- logit_bias: float32 [1], replicated, may hold values from -4 to -1
Outputs:
- loss: float32 [8], P('replica')
- grad_text: float32 [128, 1152], P(('replica', 'dp'))
- grad_tokens: bfloat16 [32768, 1152], P(('replica', 'dp'))
- grad_w_out: float32 [1152, 4304], P(('replica', 'dp'))
The draws below stay inside these ranges and needn't reach their ends.
All inputs are finite; a program needn't handle non-finite values.
Results may differ from the reference program's by a relative error of at most 0.0029.
Values may be sent and summed in bfloat16 or wider, within the bound.
A program may use at most 128 MiB of HBM per device.

```python
import jax
import jax.numpy as jnp
from jax import lax

D = 1152
FF = 4304
PATCHES = 256
S_DEV = 1
SAMPLES = 128
ROWS = 32768
N_REPLICA = 8
N_DP = 16


def level_of(rng, dims, cuts, low, high):
    factor_of, own = 1.0, jax.random.fold_in(rng, 6)
    for position, shards_of in cuts:
        steps = jnp.exp(jax.random.uniform(jax.random.fold_in(own, position), (shards_of,), jnp.float32, low / len(cuts), high / len(cuts)))
        factor_of = factor_of * jnp.repeat(steps, dims[position] // shards_of).reshape([-1 if axis == position else 1 for axis in range(len(dims))])
    return factor_of


def normal_values(stream_key, shape, spread, bound, cuts=(), kind=jnp.bfloat16):
    factor_of = level_of(stream_key, shape, cuts, -0.22, 0.18) if cuts else 1.0
    values = jax.random.normal(stream_key, shape, jnp.float32) * spread * factor_of
    return jnp.minimum(jnp.maximum(values, -bound), bound).astype(kind)


def setup_inputs(seed: int = 0) -> dict:
    key_of = jax.random.split(jax.random.key(seed), 8)
    tokens = normal_values(key_of[0], (ROWS, D), 1.0, 6.0, ((0, 128),))
    hidden = normal_values(key_of[1], (ROWS, FF), 1.0, 6.0, ((0, 128),))
    w_out = normal_values(key_of[2], (D, FF), FF ** -0.5, 0.09375)
    norm_gain = jnp.clip(1.0 + 0.18 * jax.random.normal(key_of[3], (D,), jnp.float32), 0.1, 1.9)
    text_embed = normal_values(key_of[4], (SAMPLES, D), 1.0, 6.0, ((0, 128),))
    logit_scale = jnp.clip(jax.random.uniform(key_of[5], (1,), jnp.float32, 4.0, 16.0), 4.0, 16.0)
    logit_bias = jnp.clip(jax.random.uniform(key_of[6], (1,), jnp.float32, -4.0, -1.0), -4.0, -1.0)
    return dict(tokens=tokens, hidden=hidden, w_out=w_out, norm_gain=norm_gain, text_embed=text_embed, logit_scale=logit_scale, logit_bias=logit_bias)


def reference(tokens, hidden, w_out, norm_gain, text_embed, logit_scale, logit_bias):
    group_size = S_DEV * N_DP
    group_rows = group_size * PATCHES
    tok_groups = tokens.reshape(N_REPLICA, group_rows, D)
    hid_groups = hidden.reshape(N_REPLICA, group_rows, FF)
    text_groups = text_embed.reshape(N_REPLICA, group_size, D)
    temp_scale = logit_scale[0]
    shift_bias = logit_bias[0]
    highest = lax.Precision.HIGHEST

    def visit_group(weight_total, pieces):
        tok_part, hid_part, text_part = pieces
        residual = tok_part.astype(jnp.float32) + lax.dot_general(hid_part, w_out, (((1,), (1,)), ((), ())), preferred_element_type=jnp.float32)
        row_mean = lax.optimization_barrier(jnp.mean(residual, axis=-1, keepdims=True))
        centred = residual - row_mean
        variance = lax.optimization_barrier(jnp.mean(centred * centred, axis=-1, keepdims=True))
        inv_std = 1.0 / jnp.sqrt(variance + 1e-06)
        unit_rows = centred * inv_std
        normed = unit_rows * norm_gain
        pooled = lax.optimization_barrier(jnp.mean(normed.reshape(group_size, PATCHES, D), axis=1))
        pool_norm = jnp.sqrt(lax.optimization_barrier(jnp.sum(pooled * pooled, axis=-1, keepdims=True)) + 1e-06)
        image_emb = pooled / pool_norm
        text_f32 = text_part.astype(jnp.float32)
        text_norm = jnp.sqrt(lax.optimization_barrier(jnp.sum(text_f32 * text_f32, axis=-1, keepdims=True)) + 1e-06)
        unit_text = text_f32 / text_norm
        logits = temp_scale * jnp.dot(image_emb, unit_text.T, precision=highest) + shift_bias
        label_sign = 2.0 * jnp.eye(group_size, dtype=jnp.float32) - 1.0
        loss_value = -jnp.sum(jax.nn.log_sigmoid(label_sign * logits)) / group_size
        logit_grad = -label_sign * jax.nn.sigmoid(-label_sign * logits) / group_size
        image_grad = temp_scale * jnp.dot(logit_grad, unit_text, precision=highest)
        unit_grad = temp_scale * jnp.dot(logit_grad.T, image_emb, precision=highest)
        text_grad = (unit_grad - unit_text * lax.optimization_barrier(jnp.sum(unit_text * unit_grad, axis=-1, keepdims=True))) / text_norm
        pooled_grad = (image_grad - image_emb * lax.optimization_barrier(jnp.sum(image_emb * image_grad, axis=-1, keepdims=True))) / pool_norm
        normed_grad = jnp.broadcast_to(pooled_grad[:, None, :] / PATCHES, (group_size, PATCHES, D)).reshape(group_rows, D)
        scaled_grad = normed_grad * norm_gain
        tok_grad = (scaled_grad - lax.optimization_barrier(jnp.mean(scaled_grad, axis=-1, keepdims=True)) - unit_rows * lax.optimization_barrier(jnp.mean(scaled_grad * unit_rows, axis=-1, keepdims=True))) * inv_std
        tok_grad = tok_grad.astype(jnp.bfloat16)
        weight_part = lax.dot_general(tok_grad, hid_part, (((0,), (0,)), ((), ())), preferred_element_type=jnp.float32)
        return (weight_total + weight_part, (loss_value, text_grad, tok_grad))
    weight_total, outputs = lax.scan(visit_group, jnp.zeros((D, FF), jnp.float32), (tok_groups, hid_groups, text_groups))
    losses, text_grads, tok_grads = outputs
    return (losses, text_grads.reshape(SAMPLES, D), tok_grads.reshape(ROWS, D), weight_total)
```

```python
import jax
import jax.numpy as jnp
import numpy as np
from jax import lax
from jax.experimental import pallas as pl
from jax.experimental.pallas import tpu as pltpu
from jax.sharding import PartitionSpec as P

F32 = jnp.float32
BF16 = jnp.bfloat16
MESH = pl.DeviceIdType.MESH

ROWS, D, FF = 256, 1152, 4304
GROUP = 16
HALF = 2176
HALF1 = FF - HALF
K1 = 512
K_FULL, K_TAIL = FF // K1, FF % K1
CHUNK, HALF_CHUNK = 288, 144
SUB = 72
OWN = 9

ORDERS = (("y", "z", "x"), ("z", "x", "y"), ("x", "y", "z"))
BLOCKS = (
    (0, 0, 384),
    (1, 768, 384),
    (2, 1536, 384),
    (0, 384, 384),
    (1, 1152, 384),
    (2, 1920, 256),
)


def nt(a, b):
    return lax.dot_general(a, b, (((1,), (1,)), ((), ())), preferred_element_type=F32)


def tn(a, b):
    return lax.dot_general(a, b, (((0,), (0,)), ((), ())), preferred_element_type=F32)


def row_places():
    d = np.arange(D)
    digit = {"y": d // 288, "z": d // 72 % 4, "x": d // 18 % 4}
    rest = d % 18
    return np.stack(
        [
            digit[a] * 288 + digit[b] * 72 + digit[c] * 18 + rest
            for a, b, c in ORDERS[1:]
        ]
    ).astype(np.int32)


def kernel(
    hid_hbm,
    w_hbm,
    tok_hbm,
    gain_ref,
    text_ref,
    scale_ref,
    bias_ref,
    place_ref,
    loss_ref,
    gtext_ref,
    gtok_hbm,
    gw_ref,
    w_buf,
    hid,
    tok,
    resid,
    inv_buf,
    hcols,
    g_all,
    perm,
    g_t,
    texts,
    images,
    in_sems,
    w_sems,
    out_sem,
    x_send,
    x_recv,
    t_send,
    t_recv,
    i_send,
    i_recv,
    rs_send,
    rs_recv,
    *bufs,
):
    rep = lax.axis_index("replica")
    dp = lax.axis_index("dp")
    core = lax.rem(dp, 2)
    at = {
        "x": lax.rem(lax.div(dp, 2), 4),
        "y": lax.div(rep, 2),
        "z": lax.rem(rep, 2) * 2 + lax.div(dp, 8),
    }

    def device(where, which_core):
        return (
            where["y"] * 2 + lax.div(where["z"], 2),
            lax.rem(where["z"], 2) * 8 + where["x"] * 2 + which_core,
        )

    def moved(axis, distance):
        return {**at, axis: lax.rem(at[axis] + distance, 4)}

    partner = (rep, dp + 1 - 2 * core)

    def mate(distance):
        return (rep, lax.rem(dp + distance, GROUP))

    get_hid = pltpu.make_async_copy(hid_hbm, hid, in_sems.at[0])
    get_hid.start()

    def get_w(k, size=K1):
        rows = pl.ds(pl.multiple_of(k * K1, K1), size)
        return pltpu.make_async_copy(w_hbm.at[rows], w_buf.at[rows], w_sems.at[k])

    for k in range(K_FULL):
        get_w(k).start()
    get_w(K_FULL, K_TAIL).start()
    get_tok = pltpu.make_async_copy(tok_hbm, tok, in_sems.at[1])
    get_tok.start()
    my_first = pl.multiple_of(core * HALF, 128)
    get_cols = pltpu.make_async_copy(
        hid_hbm.at[pl.ds(my_first, HALF1)],
        hcols.at[pl.ds(0, HALF1), pl.ds(0, ROWS)],
        in_sems.at[2],
    )
    get_cols.start()
    get_more = pltpu.make_async_copy(
        hid_hbm.at[pl.ds(HALF1, HALF - HALF1)],
        hcols.at[pl.ds(HALF1, HALF - HALF1), pl.ds(0, ROWS)],
        in_sems.at[3],
    )

    @pl.when(core == 0)
    def _():
        get_more.start()

    barrier = pltpu.get_barrier_semaphore()
    peers = [mate(k) for k in range(1, GROUP)]
    peers += [device(moved("y", k), c) for k in (1, 2, 3) for c in (0, 1)]
    other = 2 - 2 * lax.rem(rep, 2)
    peers += [device({**at, "z": other + k}, c) for k in (0, 1) for c in (0, 1)]
    for peer in peers:
        pl.semaphore_signal(barrier, inc=1, device_id=peer, device_id_type=MESH)

    @pl.when(core == 1)
    def _():
        hcols[HALF1:, :] = jnp.zeros((HALF - HALF1, 2 * ROWS), BF16)

    texts[dp] = text_ref[...].astype(F32)
    for k in range(2):
        place = place_ref[pl.ds(k, 1), :]

        def fill(step, _, k=k, place=place):
            first = pl.multiple_of(step * 96, 96)
            rows = lax.broadcasted_iota(jnp.int32, (96, D), 0) + first
            hot = jnp.where(rows == place, 1.0, 0.0).astype(BF16)
            perm[k, pl.ds(first, 96), :] = hot
            return 0

        lax.fori_loop(0, D // 96, fill, 0)

    get_hid.wait()
    resid[...] = jnp.zeros((ROWS, D), F32)

    def product(k, _):
        get_w(k).wait()
        rows = pl.ds(pl.multiple_of(k * K1, K1), K1)
        resid[...] += tn(hid[rows, :], w_buf[rows, :])
        return 0

    lax.fori_loop(0, K_FULL, product, 0)
    get_w(K_FULL, K_TAIL).wait()
    resid[...] += tn(hid[K_FULL * K1 :, :], w_buf[K_FULL * K1 :, :])
    get_tok.wait()

    pl.semaphore_wait(barrier, len(peers))

    def spread(buf, send, recv, k):
        return pltpu.make_async_remote_copy(
            src_ref=buf.at[dp],
            dst_ref=buf.at[dp],
            send_sem=send.at[k - 1],
            recv_sem=recv.at[k - 1],
            device_id=mate(k),
            device_id_type=MESH,
        )

    for k in range(1, GROUP):
        spread(texts, t_send, t_recv, k).start()
    their_first = pl.multiple_of((1 - core) * HALF, 128)
    swap_cols = pltpu.make_async_remote_copy(
        src_ref=hid.at[pl.ds(their_first, HALF1)],
        dst_ref=hcols.at[pl.ds(0, HALF1), pl.ds(ROWS, ROWS)],
        send_sem=x_send.at[0],
        recv_sem=x_recv.at[0],
        device_id=partner,
        device_id_type=MESH,
    )
    swap_cols.start()
    swap_more = pltpu.make_async_remote_copy(
        src_ref=hid.at[pl.ds(HALF1, HALF - HALF1)],
        dst_ref=hcols.at[pl.ds(HALF1, HALF - HALF1), pl.ds(ROWS, ROWS)],
        send_sem=x_send.at[1],
        recv_sem=x_recv.at[1],
        device_id=partner,
        device_id_type=MESH,
    )

    @pl.when(core == 1)
    def _():
        swap_more.start()

    gain = gain_ref[...]
    step_rows = 32

    def norm(step, total):
        rows = pl.ds(pl.multiple_of(step * step_rows, step_rows), step_rows)
        value = resid[rows, :] + tok[rows, :].astype(F32)
        centred = value - jnp.mean(value, axis=-1, keepdims=True)
        var = jnp.mean(centred * centred, axis=-1, keepdims=True)
        inv = 1.0 / jnp.sqrt(var + 1e-06)
        unit = centred * inv
        resid[rows, :] = unit
        inv_buf[rows, :] = jnp.broadcast_to(inv, (step_rows, 128))
        return total + jnp.sum(unit, axis=0, keepdims=True)

    total = lax.fori_loop(0, ROWS // step_rows, norm, jnp.zeros((1, D), F32))
    pooled = total * gain * (1.0 / ROWS)
    pool_norm = jnp.sqrt(jnp.sum(pooled * pooled, axis=-1, keepdims=True) + 1e-06)
    image = pooled / pool_norm
    images[dp] = image
    for k in range(1, GROUP):
        spread(images, i_send, i_recv, k).start()

    scale = scale_ref[0]
    bias = bias_ref[0]
    for k in range(1, GROUP):
        spread(texts, t_send, t_recv, k).wait_recv()
    text_rows = texts[...].reshape(GROUP, D)
    text_norm = jnp.sqrt(jnp.sum(text_rows * text_rows, axis=-1, keepdims=True) + 1e-06)
    unit_text = text_rows / text_norm
    logits = scale * jnp.sum(unit_text * image, axis=-1, keepdims=True) + bias
    is_own = lax.broadcasted_iota(jnp.int32, (GROUP, 1), 0) == dp
    sign = jnp.where(is_own, 1.0, -1.0)
    dlogit = -sign * jax.nn.sigmoid(-sign * logits) / GROUP
    dimage = scale * jnp.sum(dlogit * unit_text, axis=0, keepdims=True)
    dpooled = (
        dimage - image * jnp.sum(image * dimage, axis=-1, keepdims=True)
    ) / pool_norm
    dxhat = dpooled * (1.0 / ROWS) * gain
    centre = dxhat - jnp.mean(dxhat, axis=-1, keepdims=True)

    def token_grad(step, _):
        rows = pl.ds(pl.multiple_of(step * step_rows, step_rows), step_rows)
        unit = resid[rows, :]
        along = jnp.mean(unit * dxhat, axis=-1, keepdims=True)
        grad = (centre - unit * along) * inv_buf[rows, :1]
        g_all[rows, :] = grad.astype(BF16)
        return 0

    lax.fori_loop(0, ROWS // step_rows, token_grad, 0)
    swap_grad = pltpu.make_async_remote_copy(
        src_ref=g_all.at[pl.ds(0, ROWS)],
        dst_ref=g_all.at[pl.ds(ROWS, ROWS)],
        send_sem=x_send.at[2],
        recv_sem=x_recv.at[2],
        device_id=partner,
        device_id_type=MESH,
    )
    swap_grad.start()
    put_grad = pltpu.make_async_copy(g_all.at[pl.ds(0, ROWS)], gtok_hbm, out_sem)
    put_grad.start()
    g_t[0, :, 0:ROWS] = g_all[0:ROWS, :].T

    get_cols.wait()
    swap_cols.wait_recv()

    @pl.when(core == 0)
    def _():
        get_more.wait()
        swap_more.wait_recv()

    swap_grad.wait_recv()
    g_t[0, :, ROWS:] = g_all[ROWS:, :].T

    def buffers(b):
        return bufs[11 * b : 11 * b + 11]

    def remote(b, k, src, dst, target):
        return pltpu.make_async_remote_copy(
            src_ref=src,
            dst_ref=dst,
            send_sem=rs_send.at[b, k],
            recv_sem=rs_recv.at[b, k],
            device_id=target,
            device_id_type=MESH,
        )

    top, low = pl.ds(0, HALF_CHUNK), pl.ds(HALF_CHUNK, HALF_CHUNK)

    def first_copy(b, k):
        far, to_right, to_left, relay, fr_left, fr_right = buffers(b)[:6]
        a = ORDERS[BLOCKS[b][0]][0]
        right, left = device(moved(a, 1), core), device(moved(a, 3), core)
        src, dst, target = (
            (far.at[top], relay.at[top], right),
            (far.at[low], relay.at[low], left),
            (to_right.at[low], fr_left.at[low], right),
            (to_left.at[top], fr_right.at[top], left),
            (to_right.at[top], fr_left.at[top], right),
            (to_left.at[low], fr_right.at[low], left),
        )[k]
        return remote(b, k, src, dst, target)

    def chunk(b, distance):
        part, first, width = BLOCKS[b]
        place = lax.rem(at[ORDERS[part][0]] + distance, 4)
        rows = pl.ds(pl.multiple_of(place * CHUNK, CHUNK), CHUNK)
        if part and b < 3:
            ordered = nt(perm[part - 1, rows, :], g_all[...])
            g_t[part, rows, :] = ordered.astype(BF16)
        return nt(g_t[part, rows, :], hcols[first : first + width, :])

    def far_chunk(b):
        far = buffers(b)[0]
        far[...] = chunk(b, 2).astype(BF16)
        first_copy(b, 0).start()
        first_copy(b, 1).start()

    def near_chunks(b):
        _, to_right, to_left = buffers(b)[:3]
        hold = buffers(b)[6]
        value = chunk(b, 1)
        to_right[HALF_CHUNK:, :] = value[HALF_CHUNK:, :].astype(BF16)
        first_copy(b, 2).start()
        hold[:HALF_CHUNK, :] = value[:HALF_CHUNK, :]
        value = chunk(b, 3)
        to_left[:HALF_CHUNK, :] = value[:HALF_CHUNK, :].astype(BF16)
        first_copy(b, 3).start()
        hold[HALF_CHUNK:, :] = value[HALF_CHUNK:, :]

    def pass_on(b):
        _, to_right, to_left, relay = buffers(b)[:4]
        hold = buffers(b)[6]
        first_copy(b, 0).wait_recv()
        to_right[:HALF_CHUNK, :] = (
            hold[:HALF_CHUNK, :] + relay[:HALF_CHUNK, :].astype(F32)
        ).astype(BF16)
        first_copy(b, 4).start()
        first_copy(b, 1).wait_recv()
        to_left[HALF_CHUNK:, :] = (
            hold[HALF_CHUNK:, :] + relay[HALF_CHUNK:, :].astype(F32)
        ).astype(BF16)
        first_copy(b, 5).start()

    def own_chunk(b):
        hold = buffers(b)[6]
        hold[...] = chunk(b, 0)

    def second_copies(b):
        send2, recv2 = buffers(b)[7:9]
        axis = ORDERS[BLOCKS[b][0]][1]
        return [
            remote(
                b,
                5 + k,
                send2.at[k - 1],
                recv2.at[k - 1],
                device(moved(axis, k), core),
            )
            for k in (1, 2, 3)
        ]

    def finish_first(b):
        fr_left, fr_right, hold, send2 = buffers(b)[4:8]
        axis = ORDERS[BLOCKS[b][0]][1]
        width = BLOCKS[b][2]
        for k in (2, 3, 4, 5):
            first_copy(b, k).wait_recv()
        hold[...] = hold[...] + fr_left[...].astype(F32) + fr_right[...].astype(F32)
        for k, copy in zip((1, 2, 3), second_copies(b)):
            place = lax.rem(at[axis] + k, 4)
            rows = pl.ds(pl.multiple_of(place * SUB, SUB), SUB)
            value = jnp.concatenate([hold[rows, :], jnp.zeros((8, width), F32)], axis=0)
            send2[k - 1] = value.astype(BF16)
            copy.start()

    def third_copies(b):
        send3, recv3 = buffers(b)[9:11]
        axis = ORDERS[BLOCKS[b][0]][2]
        mine = at[axis] * 2 + core
        out = []
        for k in range(1, 8):
            there = moved(axis, k // 2)
            its_core = core if k % 2 == 0 else 1 - core
            out.append(
                remote(
                    b,
                    8 + k,
                    send3.at[there[axis] * 2 + its_core],
                    recv3.at[mine],
                    device(there, its_core),
                )
            )
        return mine, out

    def finish_second(b):
        hold = buffers(b)[6]
        recv2, send3, recv3 = buffers(b)[8:11]
        axis = ORDERS[BLOCKS[b][0]][1]
        rows = pl.ds(pl.multiple_of(at[axis] * SUB, SUB), SUB)
        value = hold[rows, :]
        for k, copy in enumerate(second_copies(b)):
            copy.wait_recv()
            value = value + recv2[k].astype(F32)[:SUB, :]
        for k in range(8):
            send3[k] = value[k * OWN : (k + 1) * OWN, :]
        mine, copies = third_copies(b)
        for copy in copies:
            copy.start()
        recv3[mine] = send3[mine]

    def finish_third(b):
        recv3 = buffers(b)[10]
        _, first, width = BLOCKS[b]
        _, copies = third_copies(b)
        for copy in copies:
            copy.wait_recv()
        for half in (0, 1):
            value = (recv3[half] + recv3[2 + half]) + (recv3[4 + half] + recv3[6 + half])
            begin = half * HALF + first
            keep = min(width, FF - begin)
            gw_ref[:, begin : begin + keep] = value[:, :keep]

    early, late = (0, 1, 2), (3, 4, 5)
    for b in early:
        far_chunk(b)
    for b in early:
        near_chunks(b)
    for b in late:
        far_chunk(b)
    for b in early:
        pass_on(b)
    for b in late:
        near_chunks(b)
    for b in early:
        own_chunk(b)
    for b in late:
        pass_on(b)
    for b in late:
        own_chunk(b)

    for k in range(1, GROUP):
        spread(images, i_send, i_recv, k).wait_recv()
    image_rows = images[...].reshape(GROUP, D)
    all_logits = (
        scale
        * lax.dot_general(
            image_rows,
            unit_text,
            (((1,), (1,)), ((), ())),
            precision=lax.Precision.HIGHEST,
            preferred_element_type=F32,
        )
        + bias
    )
    row_id = lax.broadcasted_iota(jnp.int32, (GROUP, GROUP), 0)
    col_id = lax.broadcasted_iota(jnp.int32, (GROUP, GROUP), 1)
    signed = jnp.where(row_id == col_id, all_logits, -all_logits)
    soft = jnp.minimum(signed, 0.0) - jnp.log1p(jnp.exp(-jnp.abs(signed)))
    loss_ref[0] = -jnp.sum(soft) / GROUP
    own_text = texts[dp]
    own_norm = jnp.sqrt(jnp.sum(own_text * own_text, axis=-1, keepdims=True) + 1e-06)
    own_unit = own_text / own_norm
    column = scale * jnp.sum(image_rows * own_unit, axis=-1, keepdims=True) + bias
    dcolumn = -sign * jax.nn.sigmoid(-sign * column) / GROUP
    dunit = scale * jnp.sum(dcolumn * image_rows, axis=0, keepdims=True)
    gtext_ref[...] = (
        dunit - own_unit * jnp.sum(own_unit * dunit, axis=-1, keepdims=True)
    ) / own_norm

    for b in early:
        finish_first(b)
    for b in early:
        finish_second(b)
    for b in late:
        finish_first(b)
    for b in late:
        finish_second(b)
    for b in early + late:
        finish_third(b)

    put_grad.wait()
    for k in range(1, GROUP):
        spread(texts, t_send, t_recv, k).wait_send()
        spread(images, i_send, i_recv, k).wait_send()
    swap_cols.wait_send()
    swap_grad.wait_send()

    @pl.when(core == 1)
    def _():
        swap_more.wait_send()

    for b in early + late:
        for copy in (
            [first_copy(b, k) for k in range(6)] + second_copies(b) + third_copies(b)[1]
        ):
            copy.wait_send()


def block_scratch(width):
    return [
        pltpu.VMEM((CHUNK, width), BF16),
        pltpu.VMEM((CHUNK, width), BF16),
        pltpu.VMEM((CHUNK, width), BF16),
        pltpu.VMEM((CHUNK, width), BF16),
        pltpu.VMEM((CHUNK, width), BF16),
        pltpu.VMEM((CHUNK, width), BF16),
        pltpu.VMEM((CHUNK, width), F32),
        pltpu.VMEM((3, SUB + 8, width), BF16),
        pltpu.VMEM((3, SUB + 8, width), BF16),
        pltpu.VMEM((8, OWN, width), F32),
        pltpu.VMEM((8, OWN, width), F32),
    ]


def on_device(tokens, hidden, w_out, norm_gain, text_embed, logit_scale, logit_bias):
    vmem = pl.BlockSpec(memory_space=pltpu.VMEM)
    smem = pl.BlockSpec(memory_space=pltpu.SMEM)
    anywhere = pl.BlockSpec(memory_space=pl.ANY)
    dma = pltpu.SemaphoreType.DMA
    scratch = [
        pltpu.VMEM((FF, D), BF16),
        pltpu.VMEM((FF, ROWS), BF16),
        pltpu.VMEM((ROWS, D), BF16),
        pltpu.VMEM((ROWS, D), F32),
        pltpu.VMEM((ROWS, 128), F32),
        pltpu.VMEM((HALF, 2 * ROWS), BF16),
        pltpu.VMEM((2 * ROWS, D), BF16),
        pltpu.VMEM((2, D, D), BF16),
        pltpu.VMEM((3, D, 2 * ROWS), BF16),
        pltpu.VMEM((GROUP, 1, D), F32),
        pltpu.VMEM((GROUP, 1, D), F32),
        dma((4,)),
        dma((K_FULL + 1,)),
        dma,
        dma((3,)),
        dma((3,)),
        dma((GROUP - 1,)),
        dma((GROUP - 1,)),
        dma((GROUP - 1,)),
        dma((GROUP - 1,)),
        dma((len(BLOCKS), 16)),
        dma((len(BLOCKS), 16)),
    ]
    for _, _, width in BLOCKS:
        scratch += block_scratch(width)
    return pl.pallas_call(
        kernel,
        out_shape=(
            jax.ShapeDtypeStruct((1,), F32),
            jax.ShapeDtypeStruct((1, D), F32),
            jax.ShapeDtypeStruct((ROWS, D), BF16),
            jax.ShapeDtypeStruct((OWN, FF), F32),
        ),
        in_specs=[anywhere] * 3 + [vmem] * 2 + [smem] * 2 + [vmem],
        out_specs=(smem, vmem, anywhere, vmem),
        scratch_shapes=scratch,
        compiler_params=pltpu.CompilerParams(
            collective_id=0, has_side_effects=True, vmem_limit_bytes=60 * 2**20
        ),
    )(
        hidden.T,
        w_out.T,
        tokens,
        norm_gain.reshape(1, D),
        text_embed,
        logit_scale,
        logit_bias,
        jnp.asarray(row_places()),
    )


def solution(mesh):
    rows = P(("replica", "dp"), None)
    return jax.shard_map(
        on_device,
        mesh=mesh,
        in_specs=(rows, rows, P(), P(), rows, P(), P()),
        out_specs=(P("replica"), rows, rows, rows),
        check_vma=False,
    )
```

```python
import jax
import jax.numpy as jnp
import numpy as np
from jax import lax
from jax.experimental import pallas as pl
from jax.experimental.pallas import tpu as pltpu
from jax.sharding import PartitionSpec as P

F32 = jnp.float32
BF16 = jnp.bfloat16
MESH = pl.DeviceIdType.MESH

ROWS, D, FF = 256, 1152, 4304
GROUP = 16
HALF = 2176
HALF1 = FF - HALF
K1 = 1024
BEFORE = 2
K_FULL, K_TAIL = FF // K1, FF % K1
CHUNK, HALF_CHUNK = 288, 144
SUB = 72
OWN = 9

ORDERS = (("y", "z", "x"), ("z", "x", "y"), ("x", "y", "z"))
BLOCKS = (
    (0, 0, 384),
    (1, 768, 384),
    (2, 1536, 384),
    (0, 384, 384),
    (1, 1152, 384),
    (2, 1920, 256),
)


SCHEDULE = (
    ("E", "far"),
    ("E", "near"),
    ("L", "far"),
    ("E", "pass"),
    ("L", "near"),
    ("E", "own"),
    ("L", "pass"),
    ("L", "own"),
    ("all", "loss"),
    ("E", "first"),
    ("L", "first"),
    ("E", "second"),
    ("L", "second"),
    ("E", "third"),
    ("L", "third"),
)


def nt(a, b):
    return lax.dot_general(a, b, (((1,), (1,)), ((), ())), preferred_element_type=F32)


def tn(a, b):
    return lax.dot_general(a, b, (((0,), (0,)), ((), ())), preferred_element_type=F32)


def row_places():
    d = np.arange(D)
    digit = {"y": d // 288, "z": d // 72 % 4, "x": d // 18 % 4}
    rest = d % 18
    return np.stack(
        [
            digit[a] * 288 + digit[b] * 72 + digit[c] * 18 + rest
            for a, b, c in ORDERS[1:]
        ]
    ).astype(np.int32)


def kernel(
    hid_hbm,
    w_hbm,
    tok_hbm,
    gain_hbm,
    text_hbm,
    scale_ref,
    bias_ref,
    place_hbm,
    loss_ref,
    gtext_ref,
    gtok_hbm,
    gw_ref,
    gain_ref,
    text_ref,
    place_ref,
    w_buf,
    hid,
    tok,
    resid,
    inv_buf,
    hcols,
    g_all,
    perm,
    g_t,
    texts,
    images,
    in_sems,
    w_sems,
    out_sem,
    x_send,
    x_recv,
    t_send,
    t_recv,
    i_send,
    i_recv,
    rs_send,
    rs_recv,
    *bufs,
):
    rep = lax.axis_index("replica")
    dp = lax.axis_index("dp")
    core = lax.rem(dp, 2)
    at = {
        "x": lax.rem(lax.div(dp, 2), 4),
        "y": lax.div(rep, 2),
        "z": lax.rem(rep, 2) * 2 + lax.div(dp, 8),
    }

    def device(where, which_core):
        return (
            where["y"] * 2 + lax.div(where["z"], 2),
            lax.rem(where["z"], 2) * 8 + where["x"] * 2 + which_core,
        )

    def moved(axis, distance):
        return {**at, axis: lax.rem(at[axis] + distance, 4)}

    partner = (rep, dp + 1 - 2 * core)

    def mate(distance):
        return (rep, lax.rem(dp + distance, GROUP))

    barrier = pltpu.get_barrier_semaphore()
    peers = [mate(k) for k in range(1, GROUP)]
    peers += [device(moved("y", k), c) for k in (1, 2, 3) for c in (0, 1)]
    other = 2 - 2 * lax.rem(rep, 2)
    peers += [device({**at, "z": other + k}, c) for k in (0, 1) for c in (0, 1)]
    for peer in peers:
        pl.semaphore_signal(barrier, inc=1, device_id=peer, device_id_type=MESH)

    get_small = [
        pltpu.make_async_copy(src, dst, in_sems.at[4 + k])
        for k, (src, dst) in enumerate(
            ((text_hbm, text_ref), (place_hbm, place_ref), (gain_hbm, gain_ref))
        )
    ]
    for copy in get_small:
        copy.start()
    get_hid = pltpu.make_async_copy(hid_hbm, hid, in_sems.at[0])
    get_hid.start()

    def get_w(k, size=K1):
        rows = pl.ds(pl.multiple_of(k * K1, K1), size)
        return pltpu.make_async_copy(w_hbm.at[rows], w_buf.at[rows], w_sems.at[k])

    for k in range(K_FULL):
        get_w(k).start()
    get_w(K_FULL, K_TAIL).start()
    get_tok = pltpu.make_async_copy(tok_hbm, tok, in_sems.at[1])
    get_tok.start()
    my_first = pl.multiple_of(core * HALF, 128)
    get_cols = pltpu.make_async_copy(
        hid_hbm.at[pl.ds(my_first, HALF1)],
        hcols.at[pl.ds(0, HALF1), pl.ds(0, ROWS)],
        in_sems.at[2],
    )
    get_cols.start()
    get_more = pltpu.make_async_copy(
        hid_hbm.at[pl.ds(HALF1, HALF - HALF1)],
        hcols.at[pl.ds(HALF1, HALF - HALF1), pl.ds(0, ROWS)],
        in_sems.at[3],
    )

    @pl.when(core == 0)
    def _():
        get_more.start()

    @pl.when(core == 1)
    def _():
        hcols[HALF1:, :] = jnp.zeros((HALF - HALF1, 2 * ROWS), BF16)

    for copy in get_small:
        copy.wait()
    texts[dp] = text_ref[...].astype(F32)
    for k in range(2):
        place = place_ref[pl.ds(k, 1), :]

        def fill(step, _, k=k, place=place):
            first = pl.multiple_of(step * 96, 96)
            rows = lax.broadcasted_iota(jnp.int32, (96, D), 0) + first
            hot = jnp.where(rows == place, 1.0, 0.0).astype(BF16)
            perm[k, pl.ds(first, 96), :] = hot
            return 0

        lax.fori_loop(0, D // 96, fill, 0)

    get_hid.wait()
    resid[...] = jnp.zeros((ROWS, D), F32)

    def product(k, _):
        get_w(k).wait()
        rows = pl.ds(pl.multiple_of(k * K1, K1), K1)
        resid[...] += tn(hid[rows, :], w_buf[rows, :])
        return 0

    lax.fori_loop(0, BEFORE, product, 0)

    pl.semaphore_wait(barrier, len(peers))

    def spread(buf, send, recv, k):
        return pltpu.make_async_remote_copy(
            src_ref=buf.at[dp],
            dst_ref=buf.at[dp],
            send_sem=send.at[k - 1],
            recv_sem=recv.at[k - 1],
            device_id=mate(k),
            device_id_type=MESH,
        )

    for k in range(1, GROUP):
        spread(texts, t_send, t_recv, k).start()
    their_first = pl.multiple_of((1 - core) * HALF, 128)
    swap_cols = pltpu.make_async_remote_copy(
        src_ref=hid.at[pl.ds(their_first, HALF1)],
        dst_ref=hcols.at[pl.ds(0, HALF1), pl.ds(ROWS, ROWS)],
        send_sem=x_send.at[0],
        recv_sem=x_recv.at[0],
        device_id=partner,
        device_id_type=MESH,
    )
    swap_cols.start()
    swap_more = pltpu.make_async_remote_copy(
        src_ref=hid.at[pl.ds(HALF1, HALF - HALF1)],
        dst_ref=hcols.at[pl.ds(HALF1, HALF - HALF1), pl.ds(ROWS, ROWS)],
        send_sem=x_send.at[1],
        recv_sem=x_recv.at[1],
        device_id=partner,
        device_id_type=MESH,
    )

    @pl.when(core == 1)
    def _():
        swap_more.start()

    lax.fori_loop(BEFORE, K_FULL, product, 0)
    get_w(K_FULL, K_TAIL).wait()
    resid[...] += tn(hid[K_FULL * K1 :, :], w_buf[K_FULL * K1 :, :])
    get_tok.wait()

    gain = gain_ref[...].reshape(1, D)
    step_rows = 32

    def norm(step, total):
        rows = pl.ds(pl.multiple_of(step * step_rows, step_rows), step_rows)
        value = resid[rows, :] + tok[rows, :].astype(F32)
        centred = value - jnp.mean(value, axis=-1, keepdims=True)
        var = jnp.mean(centred * centred, axis=-1, keepdims=True)
        inv = 1.0 / jnp.sqrt(var + 1e-06)
        unit = centred * inv
        resid[rows, :] = unit
        inv_buf[rows, :] = jnp.broadcast_to(inv, (step_rows, 128))
        return total + jnp.sum(unit, axis=0, keepdims=True)

    total = lax.fori_loop(0, ROWS // step_rows, norm, jnp.zeros((1, D), F32))
    pooled = total * gain * (1.0 / ROWS)
    pool_norm = jnp.sqrt(jnp.sum(pooled * pooled, axis=-1, keepdims=True) + 1e-06)
    image = pooled / pool_norm
    images[dp] = image
    for k in range(1, GROUP):
        spread(images, i_send, i_recv, k).start()

    scale = scale_ref[0]
    bias = bias_ref[0]
    for k in range(1, GROUP):
        spread(texts, t_send, t_recv, k).wait_recv()
    text_rows = texts[...].reshape(GROUP, D)
    text_norm = jnp.sqrt(jnp.sum(text_rows * text_rows, axis=-1, keepdims=True) + 1e-06)
    unit_text = text_rows / text_norm
    logits = scale * jnp.sum(unit_text * image, axis=-1, keepdims=True) + bias
    is_own = lax.broadcasted_iota(jnp.int32, (GROUP, 1), 0) == dp
    sign = jnp.where(is_own, 1.0, -1.0)
    dlogit = -sign * jax.nn.sigmoid(-sign * logits) / GROUP
    dimage = scale * jnp.sum(dlogit * unit_text, axis=0, keepdims=True)
    dpooled = (
        dimage - image * jnp.sum(image * dimage, axis=-1, keepdims=True)
    ) / pool_norm
    dxhat = dpooled * (1.0 / ROWS) * gain
    centre = dxhat - jnp.mean(dxhat, axis=-1, keepdims=True)

    def token_grad(step, _):
        rows = pl.ds(pl.multiple_of(step * step_rows, step_rows), step_rows)
        unit = resid[rows, :]
        along = jnp.mean(unit * dxhat, axis=-1, keepdims=True)
        grad = (centre - unit * along) * inv_buf[rows, :1]
        g_all[rows, :] = grad.astype(BF16)
        return 0

    lax.fori_loop(0, ROWS // step_rows, token_grad, 0)
    swap_grad = pltpu.make_async_remote_copy(
        src_ref=g_all.at[pl.ds(0, ROWS)],
        dst_ref=g_all.at[pl.ds(ROWS, ROWS)],
        send_sem=x_send.at[2],
        recv_sem=x_recv.at[2],
        device_id=partner,
        device_id_type=MESH,
    )
    swap_grad.start()
    put_grad = pltpu.make_async_copy(g_all.at[pl.ds(0, ROWS)], gtok_hbm, out_sem)
    put_grad.start()
    g_t[0, :, 0:ROWS] = g_all[0:ROWS, :].T

    get_cols.wait()
    swap_cols.wait_recv()

    @pl.when(core == 0)
    def _():
        get_more.wait()
        swap_more.wait_recv()

    swap_grad.wait_recv()
    g_t[0, :, ROWS:] = g_all[ROWS:, :].T

    def buffers(b):
        return bufs[11 * b : 11 * b + 11]

    def remote(b, k, src, dst, target):
        return pltpu.make_async_remote_copy(
            src_ref=src,
            dst_ref=dst,
            send_sem=rs_send.at[b, k],
            recv_sem=rs_recv.at[b, k],
            device_id=target,
            device_id_type=MESH,
        )

    top, low = pl.ds(0, HALF_CHUNK), pl.ds(HALF_CHUNK, HALF_CHUNK)

    def first_copy(b, k):
        far, to_right, to_left, relay, fr_left, fr_right = buffers(b)[:6]
        a = ORDERS[BLOCKS[b][0]][0]
        right, left = device(moved(a, 1), core), device(moved(a, 3), core)
        src, dst, target = (
            (far.at[top], relay.at[top], right),
            (far.at[low], relay.at[low], left),
            (to_right.at[low], fr_left.at[low], right),
            (to_left.at[top], fr_right.at[top], left),
            (to_right.at[top], fr_left.at[top], right),
            (to_left.at[low], fr_right.at[low], left),
        )[k]
        return remote(b, k, src, dst, target)

    def chunk(b, distance):
        part, first, width = BLOCKS[b]
        place = lax.rem(at[ORDERS[part][0]] + distance, 4)
        rows = pl.ds(pl.multiple_of(place * CHUNK, CHUNK), CHUNK)
        if part and b < 3:
            ordered = nt(perm[part - 1, rows, :], g_all[...])
            g_t[part, rows, :] = ordered.astype(BF16)
        return nt(g_t[part, rows, :], hcols[first : first + width, :])

    def far_chunk(b):
        far = buffers(b)[0]
        far[...] = chunk(b, 2).astype(BF16)
        first_copy(b, 0).start()
        first_copy(b, 1).start()

    def near_chunks(b):
        _, to_right, to_left = buffers(b)[:3]
        hold = buffers(b)[6]
        value = chunk(b, 1)
        to_right[HALF_CHUNK:, :] = value[HALF_CHUNK:, :].astype(BF16)
        first_copy(b, 2).start()
        hold[:HALF_CHUNK, :] = value[:HALF_CHUNK, :]
        value = chunk(b, 3)
        to_left[:HALF_CHUNK, :] = value[:HALF_CHUNK, :].astype(BF16)
        first_copy(b, 3).start()
        hold[HALF_CHUNK:, :] = value[HALF_CHUNK:, :]

    def pass_on(b):
        _, to_right, to_left, relay = buffers(b)[:4]
        hold = buffers(b)[6]
        first_copy(b, 0).wait_recv()
        to_right[:HALF_CHUNK, :] = (
            hold[:HALF_CHUNK, :] + relay[:HALF_CHUNK, :].astype(F32)
        ).astype(BF16)
        first_copy(b, 4).start()
        first_copy(b, 1).wait_recv()
        to_left[HALF_CHUNK:, :] = (
            hold[HALF_CHUNK:, :] + relay[HALF_CHUNK:, :].astype(F32)
        ).astype(BF16)
        first_copy(b, 5).start()

    def own_chunk(b):
        hold = buffers(b)[6]
        hold[...] = chunk(b, 0)

    def second_copies(b):
        send2, recv2 = buffers(b)[7:9]
        axis = ORDERS[BLOCKS[b][0]][1]
        return [
            remote(
                b,
                5 + k,
                send2.at[k - 1],
                recv2.at[k - 1],
                device(moved(axis, k), core),
            )
            for k in (1, 2, 3)
        ]

    def finish_first(b):
        fr_left, fr_right, hold, send2 = buffers(b)[4:8]
        axis = ORDERS[BLOCKS[b][0]][1]
        width = BLOCKS[b][2]
        for k in (2, 3, 4, 5):
            first_copy(b, k).wait_recv()
        hold[...] = hold[...] + fr_left[...].astype(F32) + fr_right[...].astype(F32)
        for k, copy in zip((1, 2, 3), second_copies(b)):
            place = lax.rem(at[axis] + k, 4)
            rows = pl.ds(pl.multiple_of(place * SUB, SUB), SUB)
            value = jnp.concatenate([hold[rows, :], jnp.zeros((8, width), F32)], axis=0)
            send2[k - 1] = value.astype(BF16)
            copy.start()

    def third_copies(b):
        send3, recv3 = buffers(b)[9:11]
        axis = ORDERS[BLOCKS[b][0]][2]
        mine = at[axis] * 2 + core
        out = []
        for k in range(1, 8):
            there = moved(axis, k // 2)
            its_core = core if k % 2 == 0 else 1 - core
            out.append(
                remote(
                    b,
                    8 + k,
                    send3.at[there[axis] * 2 + its_core],
                    recv3.at[mine],
                    device(there, its_core),
                )
            )
        return mine, out

    def finish_second(b):
        hold = buffers(b)[6]
        recv2, send3, recv3 = buffers(b)[8:11]
        axis = ORDERS[BLOCKS[b][0]][1]
        rows = pl.ds(pl.multiple_of(at[axis] * SUB, SUB), SUB)
        value = hold[rows, :]
        for k, copy in enumerate(second_copies(b)):
            copy.wait_recv()
            value = value + recv2[k].astype(F32)[:SUB, :]
        for k in range(8):
            send3[k] = value[k * OWN : (k + 1) * OWN, :]
        mine, copies = third_copies(b)
        for copy in copies:
            copy.start()
        recv3[mine] = send3[mine]

    def finish_third(b):
        recv3 = buffers(b)[10]
        _, first, width = BLOCKS[b]
        _, copies = third_copies(b)
        for copy in copies:
            copy.wait_recv()
        for half in (0, 1):
            value = (recv3[half] + recv3[2 + half]) + (recv3[4 + half] + recv3[6 + half])
            begin = half * HALF + first
            keep = min(width, FF - begin)
            gw_ref[:, begin : begin + keep] = value[:, :keep]

    def group_terms():
        for k in range(1, GROUP):
            spread(images, i_send, i_recv, k).wait_recv()
        image_rows = images[...].reshape(GROUP, D)
        all_logits = (
            scale
            * lax.dot_general(
                image_rows,
                unit_text,
                (((1,), (1,)), ((), ())),
                precision=lax.Precision.HIGHEST,
                preferred_element_type=F32,
            )
            + bias
        )
        row_id = lax.broadcasted_iota(jnp.int32, (GROUP, GROUP), 0)
        col_id = lax.broadcasted_iota(jnp.int32, (GROUP, GROUP), 1)
        signed = jnp.where(row_id == col_id, all_logits, -all_logits)
        soft = jnp.minimum(signed, 0.0) - jnp.log1p(jnp.exp(-jnp.abs(signed)))
        loss_ref[0] = -jnp.sum(soft) / GROUP
        own_text = texts[dp]
        own_norm = jnp.sqrt(jnp.sum(own_text * own_text, axis=-1, keepdims=True) + 1e-06)
        own_unit = own_text / own_norm
        column = scale * jnp.sum(image_rows * own_unit, axis=-1, keepdims=True) + bias
        dcolumn = -sign * jax.nn.sigmoid(-sign * column) / GROUP
        dunit = scale * jnp.sum(dcolumn * image_rows, axis=0, keepdims=True)
        gtext_ref[...] = (
            dunit - own_unit * jnp.sum(own_unit * dunit, axis=-1, keepdims=True)
        ) / own_norm

    work = {
        "far": far_chunk,
        "near": near_chunks,
        "pass": pass_on,
        "own": own_chunk,
        "first": finish_first,
        "second": finish_second,
        "third": finish_third,
    }
    for blocks, step in SCHEDULE:
        if step == "loss":
            group_terms()
        else:
            for b in (0, 1, 2) if blocks == "E" else (3, 4, 5):
                work[step](b)

    put_grad.wait()
    for k in range(1, GROUP):
        spread(texts, t_send, t_recv, k).wait_send()
        spread(images, i_send, i_recv, k).wait_send()
    swap_cols.wait_send()
    swap_grad.wait_send()

    @pl.when(core == 1)
    def _():
        swap_more.wait_send()

    for b in range(len(BLOCKS)):
        for copy in (
            [first_copy(b, k) for k in range(6)] + second_copies(b) + third_copies(b)[1]
        ):
            copy.wait_send()


def hand_over(loss, gtext, gtok, gw, loss_out, gtext_out, gtok_out, gw_out):
    loss_out[0] = loss[0]
    gtext_out[...] = gtext[...]
    gw_out[...] = gw[...]
    gtok_out[...] = gtok[...]


def block_scratch(width):
    return [
        pltpu.VMEM((CHUNK, width), BF16),
        pltpu.VMEM((CHUNK, width), BF16),
        pltpu.VMEM((CHUNK, width), BF16),
        pltpu.VMEM((CHUNK, width), BF16),
        pltpu.VMEM((CHUNK, width), BF16),
        pltpu.VMEM((CHUNK, width), BF16),
        pltpu.VMEM((CHUNK, width), F32),
        pltpu.VMEM((3, SUB + 8, width), BF16),
        pltpu.VMEM((3, SUB + 8, width), BF16),
        pltpu.VMEM((8, OWN, width), F32),
        pltpu.VMEM((8, OWN, width), F32),
    ]


def on_device(tokens, hidden, w_out, norm_gain, text_embed, logit_scale, logit_bias):
    vmem = pl.BlockSpec(memory_space=pltpu.VMEM)
    smem = pl.BlockSpec(memory_space=pltpu.SMEM)
    anywhere = pl.BlockSpec(memory_space=pl.ANY)
    dma = pltpu.SemaphoreType.DMA
    scratch = [
        pltpu.VMEM((D,), F32),
        pltpu.VMEM((1, D), BF16),
        pltpu.VMEM((2, D), jnp.int32),
        pltpu.VMEM((FF, D), BF16),
        pltpu.VMEM((FF, ROWS), BF16),
        pltpu.VMEM((ROWS, D), BF16),
        pltpu.VMEM((ROWS, D), F32),
        pltpu.VMEM((ROWS, 128), F32),
        pltpu.VMEM((HALF, 2 * ROWS), BF16),
        pltpu.VMEM((2 * ROWS, D), BF16),
        pltpu.VMEM((2, D, D), BF16),
        pltpu.VMEM((3, D, 2 * ROWS), BF16),
        pltpu.VMEM((GROUP, 1, D), F32),
        pltpu.VMEM((GROUP, 1, D), F32),
        dma((7,)),
        dma((K_FULL + 1,)),
        dma,
        dma((3,)),
        dma((3,)),
        dma((GROUP - 1,)),
        dma((GROUP - 1,)),
        dma((GROUP - 1,)),
        dma((GROUP - 1,)),
        dma((len(BLOCKS), 16)),
        dma((len(BLOCKS), 16)),
    ]
    for _, _, width in BLOCKS:
        scratch += block_scratch(width)
    made = pl.pallas_call(
        kernel,
        out_shape=(
            jax.ShapeDtypeStruct((1,), F32),
            jax.ShapeDtypeStruct((1, D), F32),
            jax.ShapeDtypeStruct((ROWS, D), BF16),
            jax.ShapeDtypeStruct((OWN, FF), F32),
        ),
        in_specs=[anywhere] * 5 + [smem] * 2 + [anywhere],
        out_specs=(smem, vmem, anywhere, vmem),
        scratch_shapes=scratch,
        compiler_params=pltpu.CompilerParams(
            collective_id=0, has_side_effects=True, vmem_limit_bytes=60 * 2**20
        ),
    )(
        hidden.T,
        w_out.T,
        tokens,
        norm_gain,
        text_embed,
        logit_scale,
        logit_bias,
        jnp.asarray(row_places()),
    )
    return pl.pallas_call(
        hand_over,
        out_shape=tuple(jax.ShapeDtypeStruct(a.shape, a.dtype) for a in made),
        in_specs=[smem, vmem, vmem, vmem],
        out_specs=(smem, vmem, vmem, vmem),
    )(*made)


def solution(mesh):
    rows = P(("replica", "dp"), None)
    return jax.shard_map(
        on_device,
        mesh=mesh,
        in_specs=(rows, rows, P(), P(), rows, P(), P()),
        out_specs=(P("replica"), rows, rows, rows),
        check_vma=False,
    )
```

```python
import jax
import jax.numpy as jnp
from jax import lax
from jax.experimental import pallas as pl
from jax.experimental.pallas import tpu as pltpu
from jax.sharding import PartitionSpec as P

F32 = jnp.float32
BF16 = jnp.bfloat16
MESH = pl.DeviceIdType.MESH

ROWS, D, FF = 256, 1152, 4304
GROUP = 16
HALF = 2176
HALF1 = FF - HALF
K1 = 1024
SWAPS = 4
BEFORE = 0
K_FULL, K_TAIL = FF // K1, FF % K1
CHUNK, HALF_CHUNK = 288, 144
SUB = 72
OWN = 9

ORDERS = (("y", "z", "x"), ("z", "x", "y"), ("x", "y", "z"))
TILES = ((3, 3, 3), (3, 3, 2))
PART_AT = (0, 768, 1536)
BLOCKS = tuple(
    (p, PART_AT[p] + 128 * sum(t[p] for t in TILES[:g]), 128 * TILES[g][p])
    for g in range(len(TILES))
    for p in range(3)
)
SCHEDULE = (
    (0, "far"),
    (0, "near"),
    (1, "far"),
    (0, "pass"),
    (1, "near"),
    (0, "own"),
    (1, "pass"),
    (1, "own"),
    (0, "loss"),
    (0, "first"),
    (1, "first"),
    (0, "second"),
    (1, "second"),
    (0, "third"),
    (1, "third"),
)


def nt(a, b):
    return lax.dot_general(a, b, (((1,), (1,)), ((), ())), preferred_element_type=F32)


def tn(a, b):
    return lax.dot_general(a, b, (((0,), (0,)), ((), ())), preferred_element_type=F32)


def row_places(order):
    rest = lax.broadcasted_iota(jnp.int32, (1, D), 1)
    digit = {}
    for axis, size in (("y", 288), ("z", 72), ("x", 18)):
        count = sum(jnp.where(rest >= k * size, 1, 0) for k in (1, 2, 3))
        rest = rest - count * size
        digit[axis] = count
    return sum(digit[axis] * size for axis, size in zip(order, (288, 72, 18))) + rest


def kernel(
    hid_hbm,
    w_hbm,
    tok_hbm,
    gain_hbm,
    text_hbm,
    scale_ref,
    bias_ref,
    loss_ref,
    gtext_ref,
    gtok_hbm,
    gw_ref,
    gain_ref,
    text_ref,
    w_buf,
    hid,
    tok,
    resid,
    inv_buf,
    hcols,
    g_all,
    perm,
    g_t,
    texts,
    images,
    in_sems,
    w_sems,
    out_sem,
    x_send,
    x_recv,
    t_send,
    t_recv,
    i_send,
    i_recv,
    rs_send,
    rs_recv,
    *bufs,
):
    rep = lax.axis_index("replica")
    dp = lax.axis_index("dp")
    core = lax.rem(dp, 2)
    at = {
        "x": lax.rem(lax.div(dp, 2), 4),
        "y": lax.div(rep, 2),
        "z": lax.rem(rep, 2) * 2 + lax.div(dp, 8),
    }

    def device(where, which_core):
        return (
            where["y"] * 2 + lax.div(where["z"], 2),
            lax.rem(where["z"], 2) * 8 + where["x"] * 2 + which_core,
        )

    def moved(axis, distance):
        return {**at, axis: lax.rem(at[axis] + distance, 4)}

    partner = (rep, dp + 1 - 2 * core)

    def mate(distance):
        return (rep, lax.rem(dp + distance, GROUP))

    barrier = pltpu.get_barrier_semaphore()
    peers = [mate(k) for k in range(1, GROUP)]
    peers += [device(moved("y", k), c) for k in (1, 2, 3) for c in (0, 1)]
    other = 2 - 2 * lax.rem(rep, 2)
    peers += [device({**at, "z": other + k}, c) for k in (0, 1) for c in (0, 1)]
    for peer in peers:
        pl.semaphore_signal(barrier, inc=1, device_id=peer, device_id_type=MESH)

    get_small = [
        pltpu.make_async_copy(src, dst, in_sems.at[4 + k])
        for k, (src, dst) in enumerate(
            ((text_hbm, text_ref), (gain_hbm, gain_ref))
        )
    ]
    for copy in get_small:
        copy.start()
    get_hid = pltpu.make_async_copy(hid_hbm, hid, in_sems.at[0])
    get_hid.start()

    def get_w(k, size=K1):
        rows = pl.ds(pl.multiple_of(k * K1, K1), size)
        return pltpu.make_async_copy(w_hbm.at[rows], w_buf.at[rows], w_sems.at[k])

    for k in range(K_FULL):
        get_w(k).start()
    get_w(K_FULL, K_TAIL).start()
    get_tok = pltpu.make_async_copy(tok_hbm, tok, in_sems.at[1])
    get_tok.start()
    my_first = pl.multiple_of(core * HALF, 128)
    get_cols = pltpu.make_async_copy(
        hid_hbm.at[pl.ds(my_first, HALF1)],
        hcols.at[pl.ds(0, HALF1), pl.ds(0, ROWS)],
        in_sems.at[2],
    )
    get_cols.start()
    get_more = pltpu.make_async_copy(
        hid_hbm.at[pl.ds(HALF1, HALF - HALF1)],
        hcols.at[pl.ds(HALF1, HALF - HALF1), pl.ds(0, ROWS)],
        in_sems.at[3],
    )

    @pl.when(core == 0)
    def _():
        get_more.start()

    @pl.when(core == 1)
    def _():
        hcols[HALF1:, :] = jnp.zeros((HALF - HALF1, 2 * ROWS), BF16)

    for copy in get_small:
        copy.wait()
    texts[dp] = text_ref[...].astype(F32)
    for k in range(2):
        place = row_places(ORDERS[1 + k])

        def fill(step, _, k=k, place=place):
            first = pl.multiple_of(step * 96, 96)
            rows = lax.broadcasted_iota(jnp.int32, (96, D), 0) + first
            hot = jnp.where(rows == place, 1.0, 0.0).astype(BF16)
            perm[k, pl.ds(first, 96), :] = hot
            return 0

        lax.fori_loop(0, D // 96, fill, 0)

    get_hid.wait()
    resid[...] = jnp.zeros((ROWS, D), F32)

    def product(k, _):
        get_w(k).wait()
        rows = pl.ds(pl.multiple_of(k * K1, K1), K1)
        resid[...] += tn(hid[rows, :], w_buf[rows, :])
        return 0

    lax.fori_loop(0, BEFORE, product, 0)

    pl.semaphore_wait(barrier, len(peers))

    def spread(buf, send, recv, k):
        return pltpu.make_async_remote_copy(
            src_ref=buf.at[dp],
            dst_ref=buf.at[dp],
            send_sem=send.at[k - 1],
            recv_sem=recv.at[k - 1],
            device_id=mate(k),
            device_id_type=MESH,
        )

    for k in range(1, GROUP):
        spread(texts, t_send, t_recv, k).start()
    their_first = pl.multiple_of((1 - core) * HALF, 128)
    swap_cols = pltpu.make_async_remote_copy(
        src_ref=hid.at[pl.ds(their_first, HALF1)],
        dst_ref=hcols.at[pl.ds(0, HALF1), pl.ds(ROWS, ROWS)],
        send_sem=x_send.at[0],
        recv_sem=x_recv.at[0],
        device_id=partner,
        device_id_type=MESH,
    )
    swap_cols.start()
    swap_more = pltpu.make_async_remote_copy(
        src_ref=hid.at[pl.ds(HALF1, HALF - HALF1)],
        dst_ref=hcols.at[pl.ds(HALF1, HALF - HALF1), pl.ds(ROWS, ROWS)],
        send_sem=x_send.at[1],
        recv_sem=x_recv.at[1],
        device_id=partner,
        device_id_type=MESH,
    )

    @pl.when(core == 1)
    def _():
        swap_more.start()

    lax.fori_loop(BEFORE, K_FULL, product, 0)
    get_w(K_FULL, K_TAIL).wait()
    resid[...] += tn(hid[K_FULL * K1 :, :], w_buf[K_FULL * K1 :, :])
    get_tok.wait()

    gain = gain_ref[...].reshape(1, D)
    step_rows = 32

    def norm(step, total):
        rows = pl.ds(pl.multiple_of(step * step_rows, step_rows), step_rows)
        value = resid[rows, :] + tok[rows, :].astype(F32)
        centred = value - jnp.mean(value, axis=-1, keepdims=True)
        var = jnp.mean(centred * centred, axis=-1, keepdims=True)
        inv = 1.0 / jnp.sqrt(var + 1e-06)
        unit = centred * inv
        resid[rows, :] = unit
        inv_buf[rows, :] = jnp.broadcast_to(inv, (step_rows, 128))
        return total + jnp.sum(unit, axis=0, keepdims=True)

    total = lax.fori_loop(0, ROWS // step_rows, norm, jnp.zeros((1, D), F32))
    pooled = total * gain * (1.0 / ROWS)
    pool_norm = jnp.sqrt(jnp.sum(pooled * pooled, axis=-1, keepdims=True) + 1e-06)
    image = pooled / pool_norm
    images[dp] = image
    for k in range(1, GROUP):
        spread(images, i_send, i_recv, k).start()

    scale = scale_ref[0]
    bias = bias_ref[0]
    for k in range(1, GROUP):
        spread(texts, t_send, t_recv, k).wait_recv()
    text_rows = texts[...].reshape(GROUP, D)
    text_norm = jnp.sqrt(jnp.sum(text_rows * text_rows, axis=-1, keepdims=True) + 1e-06)
    unit_text = text_rows / text_norm
    logits = scale * jnp.sum(unit_text * image, axis=-1, keepdims=True) + bias
    is_own = lax.broadcasted_iota(jnp.int32, (GROUP, 1), 0) == dp
    sign = jnp.where(is_own, 1.0, -1.0)
    dlogit = -sign * jax.nn.sigmoid(-sign * logits) / GROUP
    dimage = scale * jnp.sum(dlogit * unit_text, axis=0, keepdims=True)
    dpooled = (
        dimage - image * jnp.sum(image * dimage, axis=-1, keepdims=True)
    ) / pool_norm
    dxhat = dpooled * (1.0 / ROWS) * gain
    centre = dxhat - jnp.mean(dxhat, axis=-1, keepdims=True)

    def token_grad(step, _):
        rows = pl.ds(pl.multiple_of(step * step_rows, step_rows), step_rows)
        unit = resid[rows, :]
        along = jnp.mean(unit * dxhat, axis=-1, keepdims=True)
        grad = (centre - unit * along) * inv_buf[rows, :1]
        g_all[rows, :] = grad.astype(BF16)
        return 0

    def swap_grad(k):
        size = ROWS // SWAPS
        return pltpu.make_async_remote_copy(
            src_ref=g_all.at[pl.ds(k * size, size)],
            dst_ref=g_all.at[pl.ds(ROWS + k * size, size)],
            send_sem=x_send.at[2 + k],
            recv_sem=x_recv.at[2 + k],
            device_id=partner,
            device_id_type=MESH,
        )

    steps = ROWS // step_rows // SWAPS
    for k in range(SWAPS):
        lax.fori_loop(k * steps, (k + 1) * steps, token_grad, 0)
        swap_grad(k).start()
    put_grad = pltpu.make_async_copy(g_all.at[pl.ds(0, ROWS)], gtok_hbm, out_sem)
    put_grad.start()
    g_t[0, :, 0:ROWS] = g_all[0:ROWS, :].T

    get_cols.wait()
    swap_cols.wait_recv()

    @pl.when(core == 0)
    def _():
        get_more.wait()
        swap_more.wait_recv()

    for k in range(SWAPS):
        swap_grad(k).wait_recv()
    g_t[0, :, ROWS:] = g_all[ROWS:, :].T

    def buffers(b):
        return bufs[11 * b : 11 * b + 11]

    def remote(b, k, src, dst, target):
        return pltpu.make_async_remote_copy(
            src_ref=src,
            dst_ref=dst,
            send_sem=rs_send.at[b, k],
            recv_sem=rs_recv.at[b, k],
            device_id=target,
            device_id_type=MESH,
        )

    top, low = pl.ds(0, HALF_CHUNK), pl.ds(HALF_CHUNK, HALF_CHUNK)

    def first_copy(b, k):
        far, to_right, to_left, relay, fr_left, fr_right = buffers(b)[:6]
        a = ORDERS[BLOCKS[b][0]][0]
        right, left = device(moved(a, 1), core), device(moved(a, 3), core)
        src, dst, target = (
            (far.at[top], relay.at[top], right),
            (far.at[low], relay.at[low], left),
            (to_right.at[low], fr_left.at[low], right),
            (to_left.at[top], fr_right.at[top], left),
            (to_right.at[top], fr_left.at[top], right),
            (to_left.at[low], fr_right.at[low], left),
        )[k]
        return remote(b, k, src, dst, target)

    def chunk(b, distance):
        part, first, width = BLOCKS[b]
        place = lax.rem(at[ORDERS[part][0]] + distance, 4)
        rows = pl.ds(pl.multiple_of(place * CHUNK, CHUNK), CHUNK)
        if part and b < 3:
            ordered = nt(perm[part - 1, rows, :], g_all[...])
            g_t[part, rows, :] = ordered.astype(BF16)
        return nt(g_t[part, rows, :], hcols[first : first + width, :])

    def far_chunk(b):
        far = buffers(b)[0]
        far[...] = chunk(b, 2).astype(BF16)
        first_copy(b, 0).start()
        first_copy(b, 1).start()

    def near_chunks(b):
        _, to_right, to_left = buffers(b)[:3]
        hold = buffers(b)[6]
        value = chunk(b, 1)
        to_right[HALF_CHUNK:, :] = value[HALF_CHUNK:, :].astype(BF16)
        first_copy(b, 2).start()
        hold[:HALF_CHUNK, :] = value[:HALF_CHUNK, :]
        value = chunk(b, 3)
        to_left[:HALF_CHUNK, :] = value[:HALF_CHUNK, :].astype(BF16)
        first_copy(b, 3).start()
        hold[HALF_CHUNK:, :] = value[HALF_CHUNK:, :]

    def pass_on(b):
        _, to_right, to_left, relay = buffers(b)[:4]
        hold = buffers(b)[6]
        first_copy(b, 0).wait_recv()
        to_right[:HALF_CHUNK, :] = (
            hold[:HALF_CHUNK, :] + relay[:HALF_CHUNK, :].astype(F32)
        ).astype(BF16)
        first_copy(b, 4).start()
        first_copy(b, 1).wait_recv()
        to_left[HALF_CHUNK:, :] = (
            hold[HALF_CHUNK:, :] + relay[HALF_CHUNK:, :].astype(F32)
        ).astype(BF16)
        first_copy(b, 5).start()

    def own_chunk(b):
        hold = buffers(b)[6]
        hold[...] = chunk(b, 0)

    def second_copies(b):
        send2, recv2 = buffers(b)[7:9]
        axis = ORDERS[BLOCKS[b][0]][1]
        return [
            remote(
                b,
                5 + k,
                send2.at[k - 1],
                recv2.at[k - 1],
                device(moved(axis, k), core),
            )
            for k in (1, 2, 3)
        ]

    def finish_first(b):
        fr_left, fr_right, hold, send2 = buffers(b)[4:8]
        axis = ORDERS[BLOCKS[b][0]][1]
        width = BLOCKS[b][2]
        for k in (2, 3, 4, 5):
            first_copy(b, k).wait_recv()
        hold[...] = hold[...] + fr_left[...].astype(F32) + fr_right[...].astype(F32)
        for k, copy in zip((1, 2, 3), second_copies(b)):
            place = lax.rem(at[axis] + k, 4)
            rows = pl.ds(pl.multiple_of(place * SUB, SUB), SUB)
            value = jnp.concatenate([hold[rows, :], jnp.zeros((8, width), F32)], axis=0)
            send2[k - 1] = value.astype(BF16)
            copy.start()

    def third_copies(b):
        send3, recv3 = buffers(b)[9:11]
        axis = ORDERS[BLOCKS[b][0]][2]
        mine = at[axis] * 2 + core
        out = []
        for k in range(1, 8):
            there = moved(axis, k // 2)
            its_core = core if k % 2 == 0 else 1 - core
            out.append(
                remote(
                    b,
                    8 + k,
                    send3.at[there[axis] * 2 + its_core],
                    recv3.at[mine],
                    device(there, its_core),
                )
            )
        return mine, out

    def finish_second(b):
        hold = buffers(b)[6]
        recv2, send3, recv3 = buffers(b)[8:11]
        axis = ORDERS[BLOCKS[b][0]][1]
        rows = pl.ds(pl.multiple_of(at[axis] * SUB, SUB), SUB)
        value = hold[rows, :]
        for k, copy in enumerate(second_copies(b)):
            copy.wait_recv()
            value = value + recv2[k].astype(F32)[:SUB, :]
        for k in range(8):
            send3[k] = value[k * OWN : (k + 1) * OWN, :]
        mine, copies = third_copies(b)
        for copy in copies:
            copy.start()
        recv3[mine] = send3[mine]

    def finish_third(b):
        recv3 = buffers(b)[10]
        _, first, width = BLOCKS[b]
        _, copies = third_copies(b)
        for copy in copies:
            copy.wait_recv()
        for half in (0, 1):
            value = (recv3[half] + recv3[2 + half]) + (recv3[4 + half] + recv3[6 + half])
            begin = half * HALF + first
            keep = min(width, FF - begin)
            gw_ref[:, begin : begin + keep] = value[:, :keep]

    def group_terms():
        for k in range(1, GROUP):
            spread(images, i_send, i_recv, k).wait_recv()
        image_rows = images[...].reshape(GROUP, D)
        all_logits = (
            scale
            * lax.dot_general(
                image_rows,
                unit_text,
                (((1,), (1,)), ((), ())),
                precision=lax.Precision.HIGHEST,
                preferred_element_type=F32,
            )
            + bias
        )
        row_id = lax.broadcasted_iota(jnp.int32, (GROUP, GROUP), 0)
        col_id = lax.broadcasted_iota(jnp.int32, (GROUP, GROUP), 1)
        signed = jnp.where(row_id == col_id, all_logits, -all_logits)
        soft = jnp.minimum(signed, 0.0) - jnp.log1p(jnp.exp(-jnp.abs(signed)))
        loss_ref[0] = -jnp.sum(soft) / GROUP
        own_text = texts[dp]
        own_norm = jnp.sqrt(jnp.sum(own_text * own_text, axis=-1, keepdims=True) + 1e-06)
        own_unit = own_text / own_norm
        column = scale * jnp.sum(image_rows * own_unit, axis=-1, keepdims=True) + bias
        dcolumn = -sign * jax.nn.sigmoid(-sign * column) / GROUP
        dunit = scale * jnp.sum(dcolumn * image_rows, axis=0, keepdims=True)
        gtext_ref[...] = (
            dunit - own_unit * jnp.sum(own_unit * dunit, axis=-1, keepdims=True)
        ) / own_norm

    work = {
        "far": far_chunk,
        "near": near_chunks,
        "pass": pass_on,
        "own": own_chunk,
        "first": finish_first,
        "second": finish_second,
        "third": finish_third,
    }
    for group, step in SCHEDULE:
        if step == "loss":
            group_terms()
        else:
            for b in range(3 * group, 3 * group + 3):
                work[step](b)

    put_grad.wait()
    for k in range(1, GROUP):
        spread(texts, t_send, t_recv, k).wait_send()
        spread(images, i_send, i_recv, k).wait_send()
    swap_cols.wait_send()
    for k in range(SWAPS):
        swap_grad(k).wait_send()

    @pl.when(core == 1)
    def _():
        swap_more.wait_send()

    for b in range(len(BLOCKS)):
        for copy in (
            [first_copy(b, k) for k in range(6)] + second_copies(b) + third_copies(b)[1]
        ):
            copy.wait_send()


def hand_over(loss, gtext, gtok, gw, loss_out, gtext_out, gtok_out, gw_out):
    loss_out[0] = loss[0]
    gtext_out[...] = gtext[...]
    gw_out[...] = gw[...]
    gtok_out[...] = gtok[...]


def block_scratch(width):
    return [
        pltpu.VMEM((CHUNK, width), BF16),
        pltpu.VMEM((CHUNK, width), BF16),
        pltpu.VMEM((CHUNK, width), BF16),
        pltpu.VMEM((CHUNK, width), BF16),
        pltpu.VMEM((CHUNK, width), BF16),
        pltpu.VMEM((CHUNK, width), BF16),
        pltpu.VMEM((CHUNK, width), F32),
        pltpu.VMEM((3, SUB + 8, width), BF16),
        pltpu.VMEM((3, SUB + 8, width), BF16),
        pltpu.VMEM((8, OWN, width), F32),
        pltpu.VMEM((8, OWN, width), F32),
    ]


def on_device(tokens, hidden, w_out, norm_gain, text_embed, logit_scale, logit_bias):
    vmem = pl.BlockSpec(memory_space=pltpu.VMEM)
    smem = pl.BlockSpec(memory_space=pltpu.SMEM)
    anywhere = pl.BlockSpec(memory_space=pl.ANY)
    dma = pltpu.SemaphoreType.DMA
    scratch = [
        pltpu.VMEM((D,), F32),
        pltpu.VMEM((1, D), BF16),
        pltpu.VMEM((FF, D), BF16),
        pltpu.VMEM((FF, ROWS), BF16),
        pltpu.VMEM((ROWS, D), BF16),
        pltpu.VMEM((ROWS, D), F32),
        pltpu.VMEM((ROWS, 128), F32),
        pltpu.VMEM((HALF, 2 * ROWS), BF16),
        pltpu.VMEM((2 * ROWS, D), BF16),
        pltpu.VMEM((2, D, D), BF16),
        pltpu.VMEM((3, D, 2 * ROWS), BF16),
        pltpu.VMEM((GROUP, 1, D), F32),
        pltpu.VMEM((GROUP, 1, D), F32),
        dma((7,)),
        dma((K_FULL + 1,)),
        dma,
        dma((2 + SWAPS,)),
        dma((2 + SWAPS,)),
        dma((GROUP - 1,)),
        dma((GROUP - 1,)),
        dma((GROUP - 1,)),
        dma((GROUP - 1,)),
        dma((len(BLOCKS), 16)),
        dma((len(BLOCKS), 16)),
    ]
    for _, _, width in BLOCKS:
        scratch += block_scratch(width)
    made = pl.pallas_call(
        kernel,
        out_shape=(
            jax.ShapeDtypeStruct((1,), F32),
            jax.ShapeDtypeStruct((1, D), F32),
            jax.ShapeDtypeStruct((ROWS, D), BF16),
            jax.ShapeDtypeStruct((OWN, FF), F32),
        ),
        in_specs=[anywhere] * 5 + [smem] * 2,
        out_specs=(smem, vmem, anywhere, vmem),
        scratch_shapes=scratch,
        compiler_params=pltpu.CompilerParams(
            collective_id=0, has_side_effects=True, vmem_limit_bytes=60 * 2**20
        ),
    )(
        hidden.T,
        w_out.T,
        tokens,
        norm_gain,
        text_embed,
        logit_scale,
        logit_bias,
    )
    return pl.pallas_call(
        hand_over,
        out_shape=tuple(jax.ShapeDtypeStruct(a.shape, a.dtype) for a in made),
        in_specs=[smem, vmem, vmem, vmem],
        out_specs=(smem, vmem, vmem, vmem),
    )(*made)


def solution(mesh):
    rows = P(("replica", "dp"), None)
    return jax.shard_map(
        on_device,
        mesh=mesh,
        in_specs=(rows, rows, P(), P(), rows, P(), P()),
        out_specs=(P("replica"), rows, rows, rows),
        check_vma=False,
    )
```

```python
import jax
import jax.numpy as jnp
from jax import lax
from jax.experimental import pallas as pl
from jax.experimental.pallas import tpu as pltpu
from jax.sharding import PartitionSpec as P

F32 = jnp.float32
BF16 = jnp.bfloat16
MESH = pl.DeviceIdType.MESH

ROWS, D, FF = 256, 1152, 4304
GROUP = 16
HALF = 2176
HALF1 = FF - HALF
K1 = 1024
SWAPS = 4
BEFORE = 0
K_FULL, K_TAIL = FF // K1, FF % K1
CHUNK, HALF_CHUNK = 288, 144
SUB = 72
OWN = 9

ORDERS = (("y", "z", "x"), ("z", "x", "y"), ("x", "y", "z"))
TILES = ((3, 3, 3), (3, 3, 2))
PART_AT = (0, 768, 1536)
BLOCKS = tuple(
    (p, PART_AT[p] + 128 * sum(t[p] for t in TILES[:g]), 128 * TILES[g][p])
    for g in range(len(TILES))
    for p in range(3)
)
SCHEDULE = (
    (0, "far"),
    (0, "near"),
    (1, "far"),
    (0, "pass"),
    (1, "near"),
    (0, "own"),
    (1, "pass"),
    (1, "own"),
    (0, "loss"),
    (0, "first"),
    (1, "first"),
    (0, "second"),
    (1, "second"),
    (0, "third"),
    (1, "third"),
)


def nt(a, b):
    return lax.dot_general(a, b, (((1,), (1,)), ((), ())), preferred_element_type=F32)


def tn(a, b):
    return lax.dot_general(a, b, (((0,), (0,)), ((), ())), preferred_element_type=F32)


def row_places(order):
    rest = lax.broadcasted_iota(jnp.int32, (1, D), 1)
    digit = {}
    for axis, size in (("y", 288), ("z", 72), ("x", 18)):
        count = sum(jnp.where(rest >= k * size, 1, 0) for k in (1, 2, 3))
        rest = rest - count * size
        digit[axis] = count
    return sum(digit[axis] * size for axis, size in zip(order, (288, 72, 18))) + rest


def kernel(
    hid_hbm,
    w_hbm,
    tok_hbm,
    gain_hbm,
    text_hbm,
    scale_ref,
    bias_ref,
    loss_ref,
    gtext_ref,
    gtok_hbm,
    gw_ref,
    gain_ref,
    text_ref,
    w_buf,
    hid,
    tok,
    resid,
    inv_buf,
    hcols,
    g_all,
    perm,
    g_t,
    texts,
    images,
    in_sems,
    w_sems,
    out_sem,
    x_send,
    x_recv,
    t_send,
    t_recv,
    i_send,
    i_recv,
    rs_send,
    rs_recv,
    *bufs,
):
    rep = lax.axis_index("replica")
    dp = lax.axis_index("dp")
    core = lax.rem(dp, 2)
    at = {
        "x": lax.rem(lax.div(dp, 2), 4),
        "y": lax.div(rep, 2),
        "z": lax.rem(rep, 2) * 2 + lax.div(dp, 8),
    }

    def device(where, which_core):
        return (
            where["y"] * 2 + lax.div(where["z"], 2),
            lax.rem(where["z"], 2) * 8 + where["x"] * 2 + which_core,
        )

    def moved(axis, distance):
        return {**at, axis: lax.rem(at[axis] + distance, 4)}

    partner = (rep, dp + 1 - 2 * core)

    def mate(distance):
        return (rep, lax.rem(dp + distance, GROUP))

    barrier = pltpu.get_barrier_semaphore()
    peers = [mate(k) for k in range(1, GROUP)]
    peers += [device(moved("y", k), c) for k in (1, 2, 3) for c in (0, 1)]
    other = 2 - 2 * lax.rem(rep, 2)
    peers += [device({**at, "z": other + k}, c) for k in (0, 1) for c in (0, 1)]
    for peer in peers:
        pl.semaphore_signal(barrier, inc=1, device_id=peer, device_id_type=MESH)

    get_small = [
        pltpu.make_async_copy(src, dst, in_sems.at[4 + k])
        for k, (src, dst) in enumerate(
            ((text_hbm, text_ref), (gain_hbm, gain_ref))
        )
    ]
    for copy in get_small:
        copy.start()
    get_hid = pltpu.make_async_copy(hid_hbm, hid, in_sems.at[0])
    get_hid.start()

    def get_w(k, size=K1):
        rows = pl.ds(pl.multiple_of(k * K1, K1), size)
        return pltpu.make_async_copy(w_hbm.at[rows], w_buf.at[rows], w_sems.at[k])

    for k in range(K_FULL):
        get_w(k).start()
    get_w(K_FULL, K_TAIL).start()
    get_tok = pltpu.make_async_copy(tok_hbm, tok, in_sems.at[1])
    get_tok.start()
    my_first = pl.multiple_of(core * HALF, 128)
    get_cols = pltpu.make_async_copy(
        hid_hbm.at[pl.ds(my_first, HALF1)],
        hcols.at[pl.ds(0, HALF1), pl.ds(0, ROWS)],
        in_sems.at[2],
    )
    get_cols.start()
    get_more = pltpu.make_async_copy(
        hid_hbm.at[pl.ds(HALF1, HALF - HALF1)],
        hcols.at[pl.ds(HALF1, HALF - HALF1), pl.ds(0, ROWS)],
        in_sems.at[3],
    )

    @pl.when(core == 0)
    def _():
        get_more.start()

    @pl.when(core == 1)
    def _():
        hcols[HALF1:, :] = jnp.zeros((HALF - HALF1, 2 * ROWS), BF16)

    for copy in get_small:
        copy.wait()
    texts[dp] = text_ref[...].astype(F32)
    for k in range(2):
        place = row_places(ORDERS[1 + k])

        def fill(step, _, k=k, place=place):
            first = pl.multiple_of(step * 96, 96)
            rows = lax.broadcasted_iota(jnp.int32, (96, D), 0) + first
            hot = jnp.where(rows == place, 1.0, 0.0).astype(BF16)
            perm[k, pl.ds(first, 96), :] = hot
            return 0

        lax.fori_loop(0, D // 96, fill, 0)

    get_hid.wait()
    resid[...] = jnp.zeros((ROWS, D), F32)

    def product(k, _):
        get_w(k).wait()
        rows = pl.ds(pl.multiple_of(k * K1, K1), K1)
        resid[...] += tn(hid[rows, :], w_buf[rows, :])
        return 0

    lax.fori_loop(0, BEFORE, product, 0)

    pl.semaphore_wait(barrier, len(peers))

    def spread(buf, send, recv, k):
        return pltpu.make_async_remote_copy(
            src_ref=buf.at[dp],
            dst_ref=buf.at[dp],
            send_sem=send.at[k - 1],
            recv_sem=recv.at[k - 1],
            device_id=mate(k),
            device_id_type=MESH,
        )

    for k in range(1, GROUP):
        spread(texts, t_send, t_recv, k).start()
    their_first = pl.multiple_of((1 - core) * HALF, 128)
    swap_cols = pltpu.make_async_remote_copy(
        src_ref=hid.at[pl.ds(their_first, HALF1)],
        dst_ref=hcols.at[pl.ds(0, HALF1), pl.ds(ROWS, ROWS)],
        send_sem=x_send.at[0],
        recv_sem=x_recv.at[0],
        device_id=partner,
        device_id_type=MESH,
    )
    swap_cols.start()
    swap_more = pltpu.make_async_remote_copy(
        src_ref=hid.at[pl.ds(HALF1, HALF - HALF1)],
        dst_ref=hcols.at[pl.ds(HALF1, HALF - HALF1), pl.ds(ROWS, ROWS)],
        send_sem=x_send.at[1],
        recv_sem=x_recv.at[1],
        device_id=partner,
        device_id_type=MESH,
    )

    @pl.when(core == 1)
    def _():
        swap_more.start()

    lax.fori_loop(BEFORE, K_FULL, product, 0)
    get_w(K_FULL, K_TAIL).wait()
    resid[...] += tn(hid[K_FULL * K1 :, :], w_buf[K_FULL * K1 :, :])
    get_tok.wait()

    gain = gain_ref[...].reshape(1, D)
    step_rows = 32

    def norm(step, total):
        rows = pl.ds(pl.multiple_of(step * step_rows, step_rows), step_rows)
        value = resid[rows, :] + tok[rows, :].astype(F32)
        centred = value - jnp.mean(value, axis=-1, keepdims=True)
        var = jnp.mean(centred * centred, axis=-1, keepdims=True)
        inv = 1.0 / jnp.sqrt(var + 1e-06)
        unit = centred * inv
        resid[rows, :] = unit
        inv_buf[rows, :] = jnp.broadcast_to(inv, (step_rows, 128))
        return total + jnp.sum(unit, axis=0, keepdims=True)

    total = lax.fori_loop(0, ROWS // step_rows, norm, jnp.zeros((1, D), F32))
    pooled = total * gain * (1.0 / ROWS)
    pool_norm = jnp.sqrt(jnp.sum(pooled * pooled, axis=-1, keepdims=True) + 1e-06)
    image = pooled / pool_norm
    images[dp] = image
    for k in range(1, GROUP):
        spread(images, i_send, i_recv, k).start()

    scale = scale_ref[0]
    bias = bias_ref[0]
    for k in range(1, GROUP):
        spread(texts, t_send, t_recv, k).wait_recv()
    text_rows = texts[...].reshape(GROUP, D)
    text_norm = jnp.sqrt(jnp.sum(text_rows * text_rows, axis=-1, keepdims=True) + 1e-06)
    unit_text = text_rows / text_norm
    logits = scale * jnp.sum(unit_text * image, axis=-1, keepdims=True) + bias
    is_own = lax.broadcasted_iota(jnp.int32, (GROUP, 1), 0) == dp
    sign = jnp.where(is_own, 1.0, -1.0)
    dlogit = -sign * jax.nn.sigmoid(-sign * logits) / GROUP
    dimage = scale * jnp.sum(dlogit * unit_text, axis=0, keepdims=True)
    dpooled = (
        dimage - image * jnp.sum(image * dimage, axis=-1, keepdims=True)
    ) / pool_norm
    dxhat = dpooled * (1.0 / ROWS) * gain
    centre = dxhat - jnp.mean(dxhat, axis=-1, keepdims=True)

    def token_grad(step, _):
        rows = pl.ds(pl.multiple_of(step * step_rows, step_rows), step_rows)
        unit = resid[rows, :]
        along = jnp.mean(unit * dxhat, axis=-1, keepdims=True)
        grad = (centre - unit * along) * inv_buf[rows, :1]
        g_all[rows, :] = grad.astype(BF16)
        return 0

    def swap_grad(k):
        size = ROWS // SWAPS
        return pltpu.make_async_remote_copy(
            src_ref=g_all.at[pl.ds(k * size, size)],
            dst_ref=g_all.at[pl.ds(ROWS + k * size, size)],
            send_sem=x_send.at[2 + k],
            recv_sem=x_recv.at[2 + k],
            device_id=partner,
            device_id_type=MESH,
        )

    steps = ROWS // step_rows // SWAPS
    for k in range(SWAPS):
        lax.fori_loop(k * steps, (k + 1) * steps, token_grad, 0)
        swap_grad(k).start()
    put_grad = pltpu.make_async_copy(g_all.at[pl.ds(0, ROWS)], gtok_hbm, out_sem)
    put_grad.start()
    g_t[0, :, 0:ROWS] = g_all[0:ROWS, :].T

    get_cols.wait()

    @pl.when(core == 0)
    def _():
        get_more.wait()

    def buffers(b):
        return bufs[11 * b : 11 * b + 11]

    def remote(b, k, src, dst, target):
        return pltpu.make_async_remote_copy(
            src_ref=src,
            dst_ref=dst,
            send_sem=rs_send.at[b, k],
            recv_sem=rs_recv.at[b, k],
            device_id=target,
            device_id_type=MESH,
        )

    top, low = pl.ds(0, HALF_CHUNK), pl.ds(HALF_CHUNK, HALF_CHUNK)

    def first_copy(b, k):
        far, to_right, to_left, relay, fr_left, fr_right = buffers(b)[:6]
        a = ORDERS[BLOCKS[b][0]][0]
        right, left = device(moved(a, 1), core), device(moved(a, 3), core)
        src, dst, target = (
            (far.at[top], relay.at[top], right),
            (far.at[low], relay.at[low], left),
            (to_right.at[low], fr_left.at[low], right),
            (to_left.at[top], fr_right.at[top], left),
            (to_right.at[top], fr_left.at[top], right),
            (to_left.at[low], fr_right.at[low], left),
        )[k]
        return remote(b, k, src, dst, target)

    def chunk(b, distance):
        part, first, width = BLOCKS[b]
        place = lax.rem(at[ORDERS[part][0]] + distance, 4)
        rows = pl.ds(pl.multiple_of(place * CHUNK, CHUNK), CHUNK)
        if part and b < 3:
            ordered = nt(perm[part - 1, rows, :], g_all[...])
            g_t[part, rows, :] = ordered.astype(BF16)
        return nt(g_t[part, rows, :], hcols[first : first + width, :])

    def far_half(b, half):
        part, first, width = BLOCKS[b]
        place = lax.rem(at[ORDERS[part][0]] + 2, 4)
        rows = pl.ds(pl.multiple_of(place * CHUNK, CHUNK), CHUNK)
        held = pl.ds(half * ROWS, ROWS)
        if part:
            ordered = nt(perm[part - 1, rows, :], g_all[held, :])
            g_t[part, rows, held] = ordered.astype(BF16)
        return nt(g_t[part, rows, held], hcols[first : first + width, held])

    def far_chunk(b):
        far = buffers(b)[0]
        if b < 3:
            far[...] = (buffers(b)[6][...] + far_half(b, 1)).astype(BF16)
        else:
            far[...] = chunk(b, 2).astype(BF16)
        first_copy(b, 0).start()
        first_copy(b, 1).start()

    def near_chunks(b):
        _, to_right, to_left = buffers(b)[:3]
        hold = buffers(b)[6]
        value = chunk(b, 1)
        to_right[HALF_CHUNK:, :] = value[HALF_CHUNK:, :].astype(BF16)
        first_copy(b, 2).start()
        hold[:HALF_CHUNK, :] = value[:HALF_CHUNK, :]
        value = chunk(b, 3)
        to_left[:HALF_CHUNK, :] = value[:HALF_CHUNK, :].astype(BF16)
        first_copy(b, 3).start()
        hold[HALF_CHUNK:, :] = value[HALF_CHUNK:, :]

    def pass_on(b):
        _, to_right, to_left, relay = buffers(b)[:4]
        hold = buffers(b)[6]
        first_copy(b, 0).wait_recv()
        to_right[:HALF_CHUNK, :] = (
            hold[:HALF_CHUNK, :] + relay[:HALF_CHUNK, :].astype(F32)
        ).astype(BF16)
        first_copy(b, 4).start()
        first_copy(b, 1).wait_recv()
        to_left[HALF_CHUNK:, :] = (
            hold[HALF_CHUNK:, :] + relay[HALF_CHUNK:, :].astype(F32)
        ).astype(BF16)
        first_copy(b, 5).start()

    def own_chunk(b):
        hold = buffers(b)[6]
        hold[...] = chunk(b, 0)

    def second_copies(b):
        send2, recv2 = buffers(b)[7:9]
        axis = ORDERS[BLOCKS[b][0]][1]
        return [
            remote(
                b,
                5 + k,
                send2.at[k - 1],
                recv2.at[k - 1],
                device(moved(axis, k), core),
            )
            for k in (1, 2, 3)
        ]

    def finish_first(b):
        fr_left, fr_right, hold, send2 = buffers(b)[4:8]
        axis = ORDERS[BLOCKS[b][0]][1]
        width = BLOCKS[b][2]
        for k in (2, 3, 4, 5):
            first_copy(b, k).wait_recv()
        hold[...] = hold[...] + fr_left[...].astype(F32) + fr_right[...].astype(F32)
        for k, copy in zip((1, 2, 3), second_copies(b)):
            place = lax.rem(at[axis] + k, 4)
            rows = pl.ds(pl.multiple_of(place * SUB, SUB), SUB)
            value = jnp.concatenate([hold[rows, :], jnp.zeros((8, width), F32)], axis=0)
            send2[k - 1] = value.astype(BF16)
            copy.start()

    def third_copies(b):
        send3, recv3 = buffers(b)[9:11]
        axis = ORDERS[BLOCKS[b][0]][2]
        mine = at[axis] * 2 + core
        out = []
        for k in range(1, 8):
            there = moved(axis, k // 2)
            its_core = core if k % 2 == 0 else 1 - core
            out.append(
                remote(
                    b,
                    8 + k,
                    send3.at[there[axis] * 2 + its_core],
                    recv3.at[mine],
                    device(there, its_core),
                )
            )
        return mine, out

    def finish_second(b):
        hold = buffers(b)[6]
        recv2, send3, recv3 = buffers(b)[8:11]
        axis = ORDERS[BLOCKS[b][0]][1]
        rows = pl.ds(pl.multiple_of(at[axis] * SUB, SUB), SUB)
        value = hold[rows, :]
        for k, copy in enumerate(second_copies(b)):
            copy.wait_recv()
            value = value + recv2[k].astype(F32)[:SUB, :]
        for k in range(8):
            send3[k] = value[k * OWN : (k + 1) * OWN, :]
        mine, copies = third_copies(b)
        for copy in copies:
            copy.start()
        recv3[mine] = send3[mine]

    def finish_third(b):
        recv3 = buffers(b)[10]
        _, first, width = BLOCKS[b]
        _, copies = third_copies(b)
        for copy in copies:
            copy.wait_recv()
        for half in (0, 1):
            value = (recv3[half] + recv3[2 + half]) + (recv3[4 + half] + recv3[6 + half])
            begin = half * HALF + first
            keep = min(width, FF - begin)
            gw_ref[:, begin : begin + keep] = value[:, :keep]

    def group_terms():
        for k in range(1, GROUP):
            spread(images, i_send, i_recv, k).wait_recv()
        image_rows = images[...].reshape(GROUP, D)
        all_logits = (
            scale
            * lax.dot_general(
                image_rows,
                unit_text,
                (((1,), (1,)), ((), ())),
                precision=lax.Precision.HIGHEST,
                preferred_element_type=F32,
            )
            + bias
        )
        row_id = lax.broadcasted_iota(jnp.int32, (GROUP, GROUP), 0)
        col_id = lax.broadcasted_iota(jnp.int32, (GROUP, GROUP), 1)
        signed = jnp.where(row_id == col_id, all_logits, -all_logits)
        soft = jnp.minimum(signed, 0.0) - jnp.log1p(jnp.exp(-jnp.abs(signed)))
        loss_ref[0] = -jnp.sum(soft) / GROUP
        own_text = texts[dp]
        own_norm = jnp.sqrt(jnp.sum(own_text * own_text, axis=-1, keepdims=True) + 1e-06)
        own_unit = own_text / own_norm
        column = scale * jnp.sum(image_rows * own_unit, axis=-1, keepdims=True) + bias
        dcolumn = -sign * jax.nn.sigmoid(-sign * column) / GROUP
        dunit = scale * jnp.sum(dcolumn * image_rows, axis=0, keepdims=True)
        gtext_ref[...] = (
            dunit - own_unit * jnp.sum(own_unit * dunit, axis=-1, keepdims=True)
        ) / own_norm

    work = {
        "far": far_chunk,
        "near": near_chunks,
        "pass": pass_on,
        "own": own_chunk,
        "first": finish_first,
        "second": finish_second,
        "third": finish_third,
    }
    for b in range(3):
        buffers(b)[6][...] = far_half(b, 0)
    swap_cols.wait_recv()

    @pl.when(core == 0)
    def _():
        swap_more.wait_recv()

    for k in range(SWAPS):
        swap_grad(k).wait_recv()
    g_t[0, :, ROWS:] = g_all[ROWS:, :].T

    for group, step in SCHEDULE:
        if step == "loss":
            group_terms()
        else:
            for b in range(3 * group, 3 * group + 3):
                work[step](b)

    put_grad.wait()
    for k in range(1, GROUP):
        spread(texts, t_send, t_recv, k).wait_send()
        spread(images, i_send, i_recv, k).wait_send()
    swap_cols.wait_send()
    for k in range(SWAPS):
        swap_grad(k).wait_send()

    @pl.when(core == 1)
    def _():
        swap_more.wait_send()

    for b in range(len(BLOCKS)):
        for copy in (
            [first_copy(b, k) for k in range(6)] + second_copies(b) + third_copies(b)[1]
        ):
            copy.wait_send()


def hand_over(loss, gtext, gtok, gw, loss_out, gtext_out, gtok_out, gw_out):
    loss_out[0] = loss[0]
    gtext_out[...] = gtext[...]
    gw_out[...] = gw[...]
    gtok_out[...] = gtok[...]


def block_scratch(width):
    return [
        pltpu.VMEM((CHUNK, width), BF16),
        pltpu.VMEM((CHUNK, width), BF16),
        pltpu.VMEM((CHUNK, width), BF16),
        pltpu.VMEM((CHUNK, width), BF16),
        pltpu.VMEM((CHUNK, width), BF16),
        pltpu.VMEM((CHUNK, width), BF16),
        pltpu.VMEM((CHUNK, width), F32),
        pltpu.VMEM((3, SUB + 8, width), BF16),
        pltpu.VMEM((3, SUB + 8, width), BF16),
        pltpu.VMEM((8, OWN, width), F32),
        pltpu.VMEM((8, OWN, width), F32),
    ]


def on_device(tokens, hidden, w_out, norm_gain, text_embed, logit_scale, logit_bias):
    vmem = pl.BlockSpec(memory_space=pltpu.VMEM)
    smem = pl.BlockSpec(memory_space=pltpu.SMEM)
    anywhere = pl.BlockSpec(memory_space=pl.ANY)
    dma = pltpu.SemaphoreType.DMA
    scratch = [
        pltpu.VMEM((D,), F32),
        pltpu.VMEM((1, D), BF16),
        pltpu.VMEM((FF, D), BF16),
        pltpu.VMEM((FF, ROWS), BF16),
        pltpu.VMEM((ROWS, D), BF16),
        pltpu.VMEM((ROWS, D), F32),
        pltpu.VMEM((ROWS, 128), F32),
        pltpu.VMEM((HALF, 2 * ROWS), BF16),
        pltpu.VMEM((2 * ROWS, D), BF16),
        pltpu.VMEM((2, D, D), BF16),
        pltpu.VMEM((3, D, 2 * ROWS), BF16),
        pltpu.VMEM((GROUP, 1, D), F32),
        pltpu.VMEM((GROUP, 1, D), F32),
        dma((7,)),
        dma((K_FULL + 1,)),
        dma,
        dma((2 + SWAPS,)),
        dma((2 + SWAPS,)),
        dma((GROUP - 1,)),
        dma((GROUP - 1,)),
        dma((GROUP - 1,)),
        dma((GROUP - 1,)),
        dma((len(BLOCKS), 16)),
        dma((len(BLOCKS), 16)),
    ]
    for _, _, width in BLOCKS:
        scratch += block_scratch(width)
    made = pl.pallas_call(
        kernel,
        out_shape=(
            jax.ShapeDtypeStruct((1,), F32),
            jax.ShapeDtypeStruct((1, D), F32),
            jax.ShapeDtypeStruct((ROWS, D), BF16),
            jax.ShapeDtypeStruct((OWN, FF), F32),
        ),
        in_specs=[anywhere] * 5 + [smem] * 2,
        out_specs=(smem, vmem, anywhere, vmem),
        scratch_shapes=scratch,
        compiler_params=pltpu.CompilerParams(
            collective_id=0, has_side_effects=True, vmem_limit_bytes=60 * 2**20
        ),
    )(
        hidden.T,
        w_out.T,
        tokens,
        norm_gain,
        text_embed,
        logit_scale,
        logit_bias,
    )
    return pl.pallas_call(
        hand_over,
        out_shape=tuple(jax.ShapeDtypeStruct(a.shape, a.dtype) for a in made),
        in_specs=[smem, vmem, vmem, vmem],
        out_specs=(smem, vmem, vmem, vmem),
    )(*made)


def solution(mesh):
    rows = P(("replica", "dp"), None)
    return jax.shard_map(
        on_device,
        mesh=mesh,
        in_specs=(rows, rows, P(), P(), rows, P(), P()),
        out_specs=(P("replica"), rows, rows, rows),
        check_vma=False,
    )
```

```python
import jax
import jax.numpy as jnp
from jax import lax
from jax.experimental import pallas as pl
from jax.experimental.pallas import tpu as pltpu
from jax.sharding import PartitionSpec as P

F32 = jnp.float32
BF16 = jnp.bfloat16
MESH = pl.DeviceIdType.MESH

ROWS, D, FF = 256, 1152, 4304
GROUP = 16
HALF = 2176
HALF1 = FF - HALF
K1 = 1024
SWAPS = 4
BEFORE = 0
K_FULL, K_TAIL = FF // K1, FF % K1
CHUNK, HALF_CHUNK = 288, 144
SUB = 72
OWN = 9

ORDERS = (("y", "z", "x"), ("z", "x", "y"), ("x", "y", "z"))
TILES = ((3, 3, 3), (3, 3, 2))
PART_AT = (0, 768, 1536)
BLOCKS = tuple(
    (p, PART_AT[p] + 128 * sum(t[p] for t in TILES[:g]), 128 * TILES[g][p])
    for g in range(len(TILES))
    for p in range(3)
)
SCHEDULE = (
    (0, "far"),
    (0, "near"),
    (1, "far"),
    (0, "pass"),
    (1, "near"),
    (0, "own"),
    (1, "pass"),
    (1, "own"),
    (0, "loss"),
    (0, "first"),
    (1, "first"),
    (0, "second"),
    (1, "second"),
    (0, "third"),
    (1, "third"),
)


def nt(a, b):
    return lax.dot_general(a, b, (((1,), (1,)), ((), ())), preferred_element_type=F32)


def tn(a, b):
    return lax.dot_general(a, b, (((0,), (0,)), ((), ())), preferred_element_type=F32)


def row_places(order):
    rest = lax.broadcasted_iota(jnp.int32, (1, D), 1)
    digit = {}
    for axis, size in (("y", 288), ("z", 72), ("x", 18)):
        count = sum(jnp.where(rest >= k * size, 1, 0) for k in (1, 2, 3))
        rest = rest - count * size
        digit[axis] = count
    return sum(digit[axis] * size for axis, size in zip(order, (288, 72, 18))) + rest


def kernel(
    hid_hbm,
    w_hbm,
    tok_hbm,
    gain_hbm,
    text_hbm,
    scale_ref,
    bias_ref,
    loss_ref,
    gtext_ref,
    gtok_hbm,
    gw_ref,
    gain_ref,
    text_ref,
    w_buf,
    hid,
    tok,
    resid,
    inv_buf,
    hcols,
    g_all,
    perm,
    g_t,
    texts,
    images,
    in_sems,
    w_sems,
    out_sem,
    x_send,
    x_recv,
    t_send,
    t_recv,
    i_send,
    i_recv,
    rs_send,
    rs_recv,
    *bufs,
):
    rep = lax.axis_index("replica")
    dp = lax.axis_index("dp")
    core = lax.rem(dp, 2)
    at = {
        "x": lax.rem(lax.div(dp, 2), 4),
        "y": lax.div(rep, 2),
        "z": lax.rem(rep, 2) * 2 + lax.div(dp, 8),
    }

    def device(where, which_core):
        return (
            where["y"] * 2 + lax.div(where["z"], 2),
            lax.rem(where["z"], 2) * 8 + where["x"] * 2 + which_core,
        )

    def moved(axis, distance):
        return {**at, axis: lax.rem(at[axis] + distance, 4)}

    partner = (rep, dp + 1 - 2 * core)

    def mate(distance):
        return (rep, lax.rem(dp + distance, GROUP))

    barrier = pltpu.get_barrier_semaphore()
    peers = [mate(k) for k in range(1, GROUP)]
    peers += [device(moved("y", k), c) for k in (1, 2, 3) for c in (0, 1)]
    other = 2 - 2 * lax.rem(rep, 2)
    peers += [device({**at, "z": other + k}, c) for k in (0, 1) for c in (0, 1)]
    for peer in peers:
        pl.semaphore_signal(barrier, inc=1, device_id=peer, device_id_type=MESH)

    get_small = [
        pltpu.make_async_copy(src, dst, in_sems.at[4 + k])
        for k, (src, dst) in enumerate(
            ((text_hbm, text_ref), (gain_hbm, gain_ref))
        )
    ]
    for copy in get_small:
        copy.start()
    get_hid = pltpu.make_async_copy(hid_hbm, hid, in_sems.at[0])
    get_hid.start()

    def get_w(k, size=K1):
        rows = pl.ds(pl.multiple_of(k * K1, K1), size)
        return pltpu.make_async_copy(w_hbm.at[rows], w_buf.at[rows], w_sems.at[k])

    for k in range(K_FULL):
        get_w(k).start()
    get_w(K_FULL, K_TAIL).start()
    get_tok = pltpu.make_async_copy(tok_hbm, tok, in_sems.at[1])
    get_tok.start()
    my_first = pl.multiple_of(core * HALF, 128)
    get_cols = pltpu.make_async_copy(
        hid_hbm.at[pl.ds(my_first, HALF1)],
        hcols.at[pl.ds(0, HALF1), pl.ds(0, ROWS)],
        in_sems.at[2],
    )
    get_cols.start()
    get_more = pltpu.make_async_copy(
        hid_hbm.at[pl.ds(HALF1, HALF - HALF1)],
        hcols.at[pl.ds(HALF1, HALF - HALF1), pl.ds(0, ROWS)],
        in_sems.at[3],
    )

    @pl.when(core == 0)
    def _():
        get_more.start()

    @pl.when(core == 1)
    def _():
        hcols[HALF1:, :] = jnp.zeros((HALF - HALF1, 2 * ROWS), BF16)

    for copy in get_small:
        copy.wait()
    texts[dp] = text_ref[...].astype(F32)
    for k in range(2):
        place = row_places(ORDERS[1 + k])

        def fill(step, _, k=k, place=place):
            first = pl.multiple_of(step * 96, 96)
            rows = lax.broadcasted_iota(jnp.int32, (96, D), 0) + first
            hot = jnp.where(rows == place, 1.0, 0.0).astype(BF16)
            perm[k, pl.ds(first, 96), :] = hot
            return 0

        lax.fori_loop(0, D // 96, fill, 0)

    get_hid.wait()
    resid[...] = jnp.zeros((ROWS, D), F32)

    def product(k, _):
        get_w(k).wait()
        rows = pl.ds(pl.multiple_of(k * K1, K1), K1)
        resid[...] += tn(hid[rows, :], w_buf[rows, :])
        return 0

    lax.fori_loop(0, BEFORE, product, 0)

    pl.semaphore_wait(barrier, len(peers))

    def spread(buf, send, recv, k):
        return pltpu.make_async_remote_copy(
            src_ref=buf.at[dp],
            dst_ref=buf.at[dp],
            send_sem=send.at[k - 1],
            recv_sem=recv.at[k - 1],
            device_id=mate(k),
            device_id_type=MESH,
        )

    for k in range(1, GROUP):
        spread(texts, t_send, t_recv, k).start()
    their_first = pl.multiple_of((1 - core) * HALF, 128)
    swap_cols = pltpu.make_async_remote_copy(
        src_ref=hid.at[pl.ds(their_first, HALF1)],
        dst_ref=hcols.at[pl.ds(0, HALF1), pl.ds(ROWS, ROWS)],
        send_sem=x_send.at[0],
        recv_sem=x_recv.at[0],
        device_id=partner,
        device_id_type=MESH,
    )
    swap_cols.start()
    swap_more = pltpu.make_async_remote_copy(
        src_ref=hid.at[pl.ds(HALF1, HALF - HALF1)],
        dst_ref=hcols.at[pl.ds(HALF1, HALF - HALF1), pl.ds(ROWS, ROWS)],
        send_sem=x_send.at[1],
        recv_sem=x_recv.at[1],
        device_id=partner,
        device_id_type=MESH,
    )

    @pl.when(core == 1)
    def _():
        swap_more.start()

    lax.fori_loop(BEFORE, K_FULL, product, 0)
    get_w(K_FULL, K_TAIL).wait()
    resid[...] += tn(hid[K_FULL * K1 :, :], w_buf[K_FULL * K1 :, :])
    get_tok.wait()

    gain = gain_ref[...].reshape(1, D)
    step_rows = 32

    def norm(step, total):
        rows = pl.ds(pl.multiple_of(step * step_rows, step_rows), step_rows)
        value = resid[rows, :] + tok[rows, :].astype(F32)
        centred = value - jnp.mean(value, axis=-1, keepdims=True)
        var = jnp.mean(centred * centred, axis=-1, keepdims=True)
        inv = 1.0 / jnp.sqrt(var + 1e-06)
        unit = centred * inv
        resid[rows, :] = unit
        inv_buf[rows, :] = jnp.broadcast_to(inv, (step_rows, 128))
        return total + jnp.sum(unit, axis=0, keepdims=True)

    total = lax.fori_loop(0, ROWS // step_rows, norm, jnp.zeros((1, D), F32))
    pooled = total * gain * (1.0 / ROWS)
    pool_norm = jnp.sqrt(jnp.sum(pooled * pooled, axis=-1, keepdims=True) + 1e-06)
    image = pooled / pool_norm
    images[dp] = image

    scale = scale_ref[0]
    bias = bias_ref[0]
    for k in range(1, GROUP):
        spread(texts, t_send, t_recv, k).wait_recv()
    text_rows = texts[...].reshape(GROUP, D)
    text_norm = jnp.sqrt(jnp.sum(text_rows * text_rows, axis=-1, keepdims=True) + 1e-06)
    unit_text = text_rows / text_norm
    logits = scale * jnp.sum(unit_text * image, axis=-1, keepdims=True) + bias
    is_own = lax.broadcasted_iota(jnp.int32, (GROUP, 1), 0) == dp
    sign = jnp.where(is_own, 1.0, -1.0)
    dlogit = -sign * jax.nn.sigmoid(-sign * logits) / GROUP
    dimage = scale * jnp.sum(dlogit * unit_text, axis=0, keepdims=True)
    dpooled = (
        dimage - image * jnp.sum(image * dimage, axis=-1, keepdims=True)
    ) / pool_norm
    dxhat = dpooled * (1.0 / ROWS) * gain
    centre = dxhat - jnp.mean(dxhat, axis=-1, keepdims=True)

    def token_grad(step, _):
        rows = pl.ds(pl.multiple_of(step * step_rows, step_rows), step_rows)
        unit = resid[rows, :]
        along = jnp.mean(unit * dxhat, axis=-1, keepdims=True)
        grad = (centre - unit * along) * inv_buf[rows, :1]
        g_all[rows, :] = grad.astype(BF16)
        return 0

    def swap_grad(k):
        size = ROWS // SWAPS
        return pltpu.make_async_remote_copy(
            src_ref=g_all.at[pl.ds(k * size, size)],
            dst_ref=g_all.at[pl.ds(ROWS + k * size, size)],
            send_sem=x_send.at[2 + k],
            recv_sem=x_recv.at[2 + k],
            device_id=partner,
            device_id_type=MESH,
        )

    steps = ROWS // step_rows // SWAPS
    for k in range(SWAPS):
        lax.fori_loop(k * steps, (k + 1) * steps, token_grad, 0)
        swap_grad(k).start()
    put_grad = pltpu.make_async_copy(g_all.at[pl.ds(0, ROWS)], gtok_hbm, out_sem)
    put_grad.start()
    for k in range(1, GROUP):
        spread(images, i_send, i_recv, k).start()
    g_t[0, :, 0:ROWS] = g_all[0:ROWS, :].T

    get_cols.wait()
    swap_cols.wait_recv()

    @pl.when(core == 0)
    def _():
        get_more.wait()
        swap_more.wait_recv()

    for k in range(SWAPS):
        swap_grad(k).wait_recv()
    g_t[0, :, ROWS:] = g_all[ROWS:, :].T

    def buffers(b):
        return bufs[11 * b : 11 * b + 11]

    def remote(b, k, src, dst, target):
        return pltpu.make_async_remote_copy(
            src_ref=src,
            dst_ref=dst,
            send_sem=rs_send.at[b, k],
            recv_sem=rs_recv.at[b, k],
            device_id=target,
            device_id_type=MESH,
        )

    top, low = pl.ds(0, HALF_CHUNK), pl.ds(HALF_CHUNK, HALF_CHUNK)

    def first_copy(b, k):
        far, to_right, to_left, relay, fr_left, fr_right = buffers(b)[:6]
        a = ORDERS[BLOCKS[b][0]][0]
        right, left = device(moved(a, 1), core), device(moved(a, 3), core)
        src, dst, target = (
            (far.at[top], relay.at[top], right),
            (far.at[low], relay.at[low], left),
            (to_right.at[low], fr_left.at[low], right),
            (to_left.at[top], fr_right.at[top], left),
            (to_right.at[top], fr_left.at[top], right),
            (to_left.at[low], fr_right.at[low], left),
        )[k]
        return remote(b, k, src, dst, target)

    def chunk(b, distance):
        part, first, width = BLOCKS[b]
        place = lax.rem(at[ORDERS[part][0]] + distance, 4)
        rows = pl.ds(pl.multiple_of(place * CHUNK, CHUNK), CHUNK)
        if part and b < 3:
            ordered = nt(perm[part - 1, rows, :], g_all[...])
            g_t[part, rows, :] = ordered.astype(BF16)
        return nt(g_t[part, rows, :], hcols[first : first + width, :])

    def far_chunk(b):
        far = buffers(b)[0]
        far[...] = chunk(b, 2).astype(BF16)
        first_copy(b, 0).start()
        first_copy(b, 1).start()

    def near_chunks(b):
        _, to_right, to_left = buffers(b)[:3]
        hold = buffers(b)[6]
        value = chunk(b, 1)
        to_right[HALF_CHUNK:, :] = value[HALF_CHUNK:, :].astype(BF16)
        first_copy(b, 2).start()
        hold[:HALF_CHUNK, :] = value[:HALF_CHUNK, :]
        value = chunk(b, 3)
        to_left[:HALF_CHUNK, :] = value[:HALF_CHUNK, :].astype(BF16)
        first_copy(b, 3).start()
        hold[HALF_CHUNK:, :] = value[HALF_CHUNK:, :]

    def pass_on(b):
        _, to_right, to_left, relay = buffers(b)[:4]
        hold = buffers(b)[6]
        first_copy(b, 0).wait_recv()
        to_right[:HALF_CHUNK, :] = (
            hold[:HALF_CHUNK, :] + relay[:HALF_CHUNK, :].astype(F32)
        ).astype(BF16)
        first_copy(b, 4).start()
        first_copy(b, 1).wait_recv()
        to_left[HALF_CHUNK:, :] = (
            hold[HALF_CHUNK:, :] + relay[HALF_CHUNK:, :].astype(F32)
        ).astype(BF16)
        first_copy(b, 5).start()

    def own_chunk(b):
        hold = buffers(b)[6]
        hold[...] = chunk(b, 0)

    def second_copies(b):
        send2, recv2 = buffers(b)[7:9]
        axis = ORDERS[BLOCKS[b][0]][1]
        return [
            remote(
                b,
                5 + k,
                send2.at[k - 1],
                recv2.at[k - 1],
                device(moved(axis, k), core),
            )
            for k in (1, 2, 3)
        ]

    def finish_first(b):
        fr_left, fr_right, hold, send2 = buffers(b)[4:8]
        axis = ORDERS[BLOCKS[b][0]][1]
        width = BLOCKS[b][2]
        for k in (2, 3, 4, 5):
            first_copy(b, k).wait_recv()
        hold[...] = hold[...] + fr_left[...].astype(F32) + fr_right[...].astype(F32)
        for k, copy in zip((1, 2, 3), second_copies(b)):
            place = lax.rem(at[axis] + k, 4)
            rows = pl.ds(pl.multiple_of(place * SUB, SUB), SUB)
            value = jnp.concatenate([hold[rows, :], jnp.zeros((8, width), F32)], axis=0)
            send2[k - 1] = value.astype(BF16)
            copy.start()

    def third_copies(b):
        send3, recv3 = buffers(b)[9:11]
        axis = ORDERS[BLOCKS[b][0]][2]
        mine = at[axis] * 2 + core
        out = []
        for k in range(1, 8):
            there = moved(axis, k // 2)
            its_core = core if k % 2 == 0 else 1 - core
            out.append(
                remote(
                    b,
                    8 + k,
                    send3.at[there[axis] * 2 + its_core],
                    recv3.at[mine],
                    device(there, its_core),
                )
            )
        return mine, out

    def finish_second(b):
        hold = buffers(b)[6]
        recv2, send3, recv3 = buffers(b)[8:11]
        axis = ORDERS[BLOCKS[b][0]][1]
        rows = pl.ds(pl.multiple_of(at[axis] * SUB, SUB), SUB)
        value = hold[rows, :]
        for k, copy in enumerate(second_copies(b)):
            copy.wait_recv()
            value = value + recv2[k].astype(F32)[:SUB, :]
        for k in range(8):
            send3[k] = value[k * OWN : (k + 1) * OWN, :]
        mine, copies = third_copies(b)
        for copy in copies:
            copy.start()
        recv3[mine] = send3[mine]

    def finish_third(b):
        recv3 = buffers(b)[10]
        _, first, width = BLOCKS[b]
        _, copies = third_copies(b)
        for copy in copies:
            copy.wait_recv()
        for half in (0, 1):
            value = (recv3[half] + recv3[2 + half]) + (recv3[4 + half] + recv3[6 + half])
            begin = half * HALF + first
            keep = min(width, FF - begin)
            gw_ref[:, begin : begin + keep] = value[:, :keep]

    def group_terms():
        for k in range(1, GROUP):
            spread(images, i_send, i_recv, k).wait_recv()
        image_rows = images[...].reshape(GROUP, D)
        all_logits = (
            scale
            * lax.dot_general(
                image_rows,
                unit_text,
                (((1,), (1,)), ((), ())),
                precision=lax.Precision.HIGHEST,
                preferred_element_type=F32,
            )
            + bias
        )
        row_id = lax.broadcasted_iota(jnp.int32, (GROUP, GROUP), 0)
        col_id = lax.broadcasted_iota(jnp.int32, (GROUP, GROUP), 1)
        signed = jnp.where(row_id == col_id, all_logits, -all_logits)
        soft = jnp.minimum(signed, 0.0) - jnp.log1p(jnp.exp(-jnp.abs(signed)))
        loss_ref[0] = -jnp.sum(soft) / GROUP
        own_text = texts[dp]
        own_norm = jnp.sqrt(jnp.sum(own_text * own_text, axis=-1, keepdims=True) + 1e-06)
        own_unit = own_text / own_norm
        column = scale * jnp.sum(image_rows * own_unit, axis=-1, keepdims=True) + bias
        dcolumn = -sign * jax.nn.sigmoid(-sign * column) / GROUP
        dunit = scale * jnp.sum(dcolumn * image_rows, axis=0, keepdims=True)
        gtext_ref[...] = (
            dunit - own_unit * jnp.sum(own_unit * dunit, axis=-1, keepdims=True)
        ) / own_norm

    work = {
        "far": far_chunk,
        "near": near_chunks,
        "pass": pass_on,
        "own": own_chunk,
        "first": finish_first,
        "second": finish_second,
        "third": finish_third,
    }
    for group, step in SCHEDULE:
        if step == "loss":
            group_terms()
        else:
            for b in range(3 * group, 3 * group + 3):
                work[step](b)

    put_grad.wait()
    for k in range(1, GROUP):
        spread(texts, t_send, t_recv, k).wait_send()
        spread(images, i_send, i_recv, k).wait_send()
    swap_cols.wait_send()
    for k in range(SWAPS):
        swap_grad(k).wait_send()

    @pl.when(core == 1)
    def _():
        swap_more.wait_send()

    for b in range(len(BLOCKS)):
        for copy in (
            [first_copy(b, k) for k in range(6)] + second_copies(b) + third_copies(b)[1]
        ):
            copy.wait_send()


def hand_over(loss, gtext, gtok, gw, loss_out, gtext_out, gtok_out, gw_out):
    loss_out[0] = loss[0]
    gtext_out[...] = gtext[...]
    gw_out[...] = gw[...]
    gtok_out[...] = gtok[...]


def block_scratch(width):
    return [
        pltpu.VMEM((CHUNK, width), BF16),
        pltpu.VMEM((CHUNK, width), BF16),
        pltpu.VMEM((CHUNK, width), BF16),
        pltpu.VMEM((CHUNK, width), BF16),
        pltpu.VMEM((CHUNK, width), BF16),
        pltpu.VMEM((CHUNK, width), BF16),
        pltpu.VMEM((CHUNK, width), F32),
        pltpu.VMEM((3, SUB + 8, width), BF16),
        pltpu.VMEM((3, SUB + 8, width), BF16),
        pltpu.VMEM((8, OWN, width), F32),
        pltpu.VMEM((8, OWN, width), F32),
    ]


def on_device(tokens, hidden, w_out, norm_gain, text_embed, logit_scale, logit_bias):
    vmem = pl.BlockSpec(memory_space=pltpu.VMEM)
    smem = pl.BlockSpec(memory_space=pltpu.SMEM)
    anywhere = pl.BlockSpec(memory_space=pl.ANY)
    dma = pltpu.SemaphoreType.DMA
    scratch = [
        pltpu.VMEM((D,), F32),
        pltpu.VMEM((1, D), BF16),
        pltpu.VMEM((FF, D), BF16),
        pltpu.VMEM((FF, ROWS), BF16),
        pltpu.VMEM((ROWS, D), BF16),
        pltpu.VMEM((ROWS, D), F32),
        pltpu.VMEM((ROWS, 128), F32),
        pltpu.VMEM((HALF, 2 * ROWS), BF16),
        pltpu.VMEM((2 * ROWS, D), BF16),
        pltpu.VMEM((2, D, D), BF16),
        pltpu.VMEM((3, D, 2 * ROWS), BF16),
        pltpu.VMEM((GROUP, 1, D), F32),
        pltpu.VMEM((GROUP, 1, D), F32),
        dma((7,)),
        dma((K_FULL + 1,)),
        dma,
        dma((2 + SWAPS,)),
        dma((2 + SWAPS,)),
        dma((GROUP - 1,)),
        dma((GROUP - 1,)),
        dma((GROUP - 1,)),
        dma((GROUP - 1,)),
        dma((len(BLOCKS), 16)),
        dma((len(BLOCKS), 16)),
    ]
    for _, _, width in BLOCKS:
        scratch += block_scratch(width)
    made = pl.pallas_call(
        kernel,
        out_shape=(
            jax.ShapeDtypeStruct((1,), F32),
            jax.ShapeDtypeStruct((1, D), F32),
            jax.ShapeDtypeStruct((ROWS, D), BF16),
            jax.ShapeDtypeStruct((OWN, FF), F32),
        ),
        in_specs=[anywhere] * 5 + [smem] * 2,
        out_specs=(smem, vmem, anywhere, vmem),
        scratch_shapes=scratch,
        compiler_params=pltpu.CompilerParams(
            collective_id=0, has_side_effects=True, vmem_limit_bytes=60 * 2**20
        ),
    )(
        hidden.T,
        w_out.T,
        tokens,
        norm_gain,
        text_embed,
        logit_scale,
        logit_bias,
    )
    return pl.pallas_call(
        hand_over,
        out_shape=tuple(jax.ShapeDtypeStruct(a.shape, a.dtype) for a in made),
        in_specs=[smem, vmem, vmem, vmem],
        out_specs=(smem, vmem, vmem, vmem),
    )(*made)


def solution(mesh):
    rows = P(("replica", "dp"), None)
    return jax.shard_map(
        on_device,
        mesh=mesh,
        in_specs=(rows, rows, P(), P(), rows, P(), P()),
        out_specs=(P("replica"), rows, rows, rows),
        check_vma=False,
    )
```
